128 devices in a mesh: dp: 8 (over x, core), expert: 16 (over z, y).
Axes of the slice: x: 4, y: 4, z: 4, core: 2. Of those that a mesh axis runs over, the one named last changes fastest.
Arguments:
- activations: bfloat16 [16384, 2048], P(('dp', 'expert')), may hold values from -6 to 6
- out_grad: bfloat16 [16384, 2048], P(('dp', 'expert')), may hold values from -4 to 4
- gate_probs: bfloat16 [16384, 8], P(('dp', 'expert')), may hold values from 0.019897461 to 0.29882812
- expert_ids: int32 [16384, 8], P('dp'), may hold values from 0 to 31, all different within a row; in each aligned block of 128 rows (0 to 127, 128 to 255, ...) at most 48 rows name the same one
- w_gate: bfloat16 [32, 2048, 512], P('expert'), may hold values from -0.125 to 0.125
- w_up: bfloat16 [32, 2048, 512], P('expert'), may hold values from -0.125 to 0.125
- w_down: bfloat16 [32, 512, 2048], P('expert'), may hold values from -0.25 to 0.25
Outputs:
- grad_act: bfloat16 [16384, 2048], P(('dp', 'expert'))
- grad_prob: float32 [16384, 8], P(('dp', 'expert'))
- grad_gate: bfloat16 [32, 2048, 512], P('expert', 'dp')
- grad_up: bfloat16 [32, 2048, 512], P('expert', 'dp')
- grad_down: bfloat16 [32, 512, 2048], P('expert', 'dp')
The draws below stay inside these ranges and needn't reach their ends.
Inputs may be any that keep to these rules, and one draw needn't show every extreme that they name: `expert_ids`: each row names 8 different experts. In every aligned block of 128 rows (the tokens of one device) no expert is named by more than 48 rows, and in some blocks one is named by exactly 48 rows.
All inputs are finite; a program needn't handle non-finite values.
Results may differ from the reference program's by a relative error of at most 0.017.
Values may be sent and summed in bfloat16 or wider, within the bound.
No kernel may reach another device: no remote copies, remote signals or barrier semaphores. Data moves between devices by JAX's collectives and lax.ppermute only.
A program may use at most 192 MiB of HBM per device.

```python
import math
import jax
import jax.numpy as jnp
import numpy as np
from jax import lax

D = 2048
FF = 512
TOP = 8
EXP_DEV = 2
TOK_DEV = 128
EXPERTS = 32
TOKENS = 16384
PEER = 48
N_DP = 8
N_EXPERT = 16


def steps_of(stream_key, dims, cuts, least, high):
    def one(axis_at, shards_of):
        draws = jax.random.uniform(jax.random.fold_in(jax.random.fold_in(stream_key, 6), axis_at), (shards_of,), jnp.float32, least / len(cuts), high / len(cuts))
        return jnp.repeat(jnp.exp(draws), dims[axis_at] // shards_of).reshape((-1,) + (1,) * (len(dims) - axis_at - 1))

    factor_of = one(*cuts[0])
    for cut in cuts[1:]:
        factor_of = factor_of * one(*cut)
    return factor_of


def routed_block(stream_key, own, number, rows, count, top, limit, slope):
    ranking = jax.random.permutation(stream_key, count)
    packed, ordinary = load_shares(count, rows * top, limit, slope, True), load_shares(count, rows * top, limit, slope, False)
    places = jnp.arange(count)

    def named(sizes, offset_by):
        used = int((sizes > 0).sum())
        fixed = max(1, used // 4)
        shifted = fixed + (places - fixed + offset_by * (used - fixed)) % max(1, count - fixed)
        return jnp.zeros((count,), jnp.int32).at[ranking[jnp.where(places < fixed, places, shifted)]].set(jnp.asarray(sizes, jnp.int32))

    sizes = jnp.where(number % 4 == 0, named(packed, number // 4), named(ordinary, number - number // 4 - 1))
    mixed = jax.random.permutation(jax.random.fold_in(own, 3), count)
    donor, taker = mixed[0:count // 2 * 2:2], mixed[1:count // 2 * 2:2]
    slack = jnp.minimum(sizes[donor] - 1, limit - sizes[taker]) // 2
    slack = jnp.where((donor == ranking[0]) | (taker == ranking[0]) | (sizes[taker] == 0), 0, jnp.maximum(slack, 0))
    shifted = jax.random.randint(jax.random.fold_in(own, 4), (count // 2,), 0, 1 << 20) % (slack + 1)
    sizes = sizes.at[donor].add(-shifted).at[taker].add(shifted)
    items = jnp.searchsorted(jnp.cumsum(sizes), jnp.arange(rows * top), side="right").astype(jnp.int32)
    listing = items.reshape(top, rows).T
    listing = listing[jax.random.permutation(jax.random.fold_in(own, 1), rows)]
    offset_by = jax.random.randint(jax.random.fold_in(own, 2), (rows, 1), 0, top)
    return jnp.take_along_axis(listing, (jnp.arange(top)[None, :] + offset_by) % top, axis=1)


def load_shares(amount, total, most, skew, full):
    weights = [(1 << 20) // math.isqrt(standing ** skew) + 1 for standing in range(1, amount + 1)]
    largest = most if full else min(most, max(-(-total // amount), total * weights[0] // sum(weights)))
    least = 1 if total - largest >= amount - 1 else 0
    given, surplus = [largest] + [least] * (amount - 1), total - largest - least * (amount - 1)
    while surplus > 0:
        candidates = [i for i in range(1, amount) if given[i] < largest] or [i for i in range(1, amount) if given[i] < most]
        mass, remaining = sum([weights[i] for i in candidates]), surplus
        for i in candidates:
            more = min(most - given[i], max(1, remaining * weights[i] // mass), surplus)
            given[i] = given[i] + more
            surplus = surplus - more
    return np.array(given)


def noise(key, dims, width, most, cuts=(), kind=jnp.bfloat16):
    entries = jax.random.normal(key, dims, jnp.float32) * width
    if len(cuts) > 0:
        entries = steps_of(key, dims, cuts, -0.22, 0.18) * entries
    return jnp.clip(entries, min=-most, max=most).astype(kind)


def setup_inputs(seed: int = 0) -> dict:
    arg_keys = jax.random.split(jax.random.key(seed), 8)
    activations = noise(arg_keys[0], (TOKENS, D), 1.0, 6.0, ((0, 128),))
    out_grad = noise(arg_keys[1], (TOKENS, D), 0.5, 4.0, ((0, 128),))
    gate_probs = jnp.clip(0.019897461 + 0.27893066 * jax.random.uniform(arg_keys[2], (TOKENS, TOP), jnp.float32) ** steps_of(arg_keys[2], (TOKENS, TOP), ((0, 128),), -0.2, 0.2), 0.019897461, 0.29882812).astype(jnp.bfloat16)
    expert_ids_keys = jax.random.split(jax.random.fold_in(arg_keys[3], 1), TOKENS // TOK_DEV)
    expert_ids_turns = jax.random.permutation(jax.random.fold_in(arg_keys[3], 3), TOKENS // TOK_DEV)
    expert_ids = jax.vmap(lambda own, number: routed_block(jax.random.fold_in(arg_keys[3], 2), own, number, TOK_DEV, EXPERTS, TOP, PEER, 2))(expert_ids_keys, expert_ids_turns).reshape((TOKENS, TOP))
    w_gate = noise(arg_keys[4], (EXPERTS, D, FF), D ** -0.5, 0.125, ((0, 16),))
    w_up = noise(arg_keys[5], (EXPERTS, D, FF), D ** -0.5, 0.125, ((0, 16),))
    w_down = noise(arg_keys[6], (EXPERTS, FF, D), FF ** -0.5, 0.25, ((0, 16),))
    return dict(activations=activations, out_grad=out_grad, gate_probs=gate_probs, expert_ids=expert_ids, w_gate=w_gate, w_up=w_up, w_down=w_down)


def to_half(value):
    return lax.optimization_barrier(value.astype(jnp.bfloat16)).astype(jnp.float32)


def slot_table(routes, experts, tok_dev, peer_slots):
    hit_count = jnp.sum((routes[:, :, None] == experts[None, None, :]).astype(jnp.int32), axis=1)
    blocks = routes.shape[0] // tok_dev
    hit_count = hit_count.reshape(blocks, tok_dev, -1)
    slot_rank = jnp.cumsum(hit_count, axis=1) - hit_count
    counts = jnp.sum(hit_count, axis=1)
    target = jnp.where(hit_count > 0, slot_rank, peer_slots)
    places = jnp.arange(peer_slots, dtype=jnp.int32)
    local_rows = jnp.arange(tok_dev, dtype=jnp.int32)
    slot_token = jnp.sum(jnp.where(target[:, :, :, None] == places[None, None, None, :], local_rows[None, :, None, None], jnp.int32(0)), axis=1)
    slot_token = slot_token + (jnp.arange(blocks, dtype=jnp.int32) * tok_dev)[:, None, None]
    live_slot = places[None, None, :] < counts[:, :, None]
    expert_count = experts.shape[0]
    slot_token = jnp.transpose(slot_token, (1, 0, 2)).reshape(expert_count, blocks * peer_slots)
    live_slot = jnp.transpose(live_slot, (1, 0, 2)).reshape(expert_count, blocks * peer_slots)
    return slot_token.astype(jnp.int32), live_slot


def mix(form, left, right):
    return jnp.einsum(form, left.astype(jnp.float32), right.astype(jnp.float32), precision=lax.Precision.HIGHEST)


def expert_pass(rows_x, rows_dy, slot_gate, gate_w, up_w, down_w):
    pre_gate = mix("ecd,edf->ecf", rows_x, gate_w)
    pre_up = mix("ecd,edf->ecf", rows_x, up_w)
    sigmoid_gate = jax.nn.sigmoid(pre_gate)
    hidden_act = to_half(pre_gate * sigmoid_gate * pre_up)
    expert_out = mix("ecf,efd->ecd", hidden_act, down_w)
    slot_dot = jnp.einsum("ecd,ecd->ec", rows_dy.astype(jnp.float32), expert_out, precision=lax.Precision.HIGHEST)
    scaled = to_half(slot_gate[:, :, None] * rows_dy.astype(jnp.float32))
    hidden_grad = mix("ecd,efd->ecf", scaled, down_w)
    gate_grad = to_half(hidden_grad * pre_up * sigmoid_gate * (1.0 + pre_gate * (1.0 - sigmoid_gate)))
    up_grad = to_half(hidden_grad * pre_gate * sigmoid_gate)
    sum_down = mix("ecf,ecd->efd", hidden_act, scaled)
    sum_gate = mix("ecd,ecf->edf", rows_x, gate_grad)
    sum_up = mix("ecd,ecf->edf", rows_x, up_grad)
    row_grad = mix("ecf,edf->ecd", gate_grad, gate_w) + mix("ecf,edf->ecd", up_grad, up_w)
    return slot_dot, row_grad, sum_gate, sum_up, sum_down


def reference(activations, out_grad, gate_probs, expert_ids, w_gate, w_up, w_down):
    group_rows = TOK_DEV * N_EXPERT
    inputs = (activations.reshape(N_DP, group_rows, D), out_grad.reshape(N_DP, group_rows, D),
              gate_probs.reshape(N_DP, group_rows, TOP), expert_ids.reshape(N_DP, group_rows, TOP))

    def one_group(weight_sums, pieces):
        x_grp, dy_grp, prob_grp, id_grp = pieces

        def one_device(carry, dev_index):
            act_sum, prob_sum = carry
            my_experts = dev_index * EXP_DEV + jnp.arange(EXP_DEV, dtype=jnp.int32)
            slot_token, live_slot = slot_table(id_grp, my_experts, TOK_DEV, PEER)
            expert_lane = jnp.broadcast_to(jnp.arange(EXP_DEV, dtype=jnp.int32)[:, None], slot_token.shape)
            group_sel = jnp.sum(jnp.where(id_grp[:, :, None] == my_experts[None, None, :], prob_grp.astype(jnp.float32)[:, :, None], 0.0), axis=1)
            slot_gate = jnp.where(live_slot, group_sel[slot_token, expert_lane], 0.0)
            gate_w = lax.dynamic_slice_in_dim(w_gate, dev_index * EXP_DEV, EXP_DEV, 0)
            up_w = lax.dynamic_slice_in_dim(w_up, dev_index * EXP_DEV, EXP_DEV, 0)
            down_w = lax.dynamic_slice_in_dim(w_down, dev_index * EXP_DEV, EXP_DEV, 0)
            slot_dot, row_grad, sum_gate, sum_up, sum_down = expert_pass(x_grp[slot_token], dy_grp[slot_token], slot_gate, gate_w, up_w, down_w)
            act_part = jnp.zeros((group_rows, D), jnp.float32).at[slot_token.reshape(-1)].add(row_grad.reshape(-1, D))
            prob_cols = jnp.zeros((group_rows, EXP_DEV), jnp.float32).at[slot_token, expert_lane].add(jnp.where(live_slot, slot_dot, 0.0))
            prob_part = jnp.sum(jnp.where(id_grp[:, :, None] == my_experts[None, None, :], prob_cols[:, None, :], 0.0), axis=2)
            return (act_sum + to_half(act_part), prob_sum + prob_part), (sum_gate, sum_up, sum_down)

        start = (jnp.zeros((group_rows, D), jnp.float32), jnp.zeros((group_rows, TOP), jnp.float32))
        (act_sum, prob_sum), grads = lax.scan(one_device, start, jnp.arange(N_EXPERT, dtype=jnp.int32))
        gate_sum = weight_sums[0] + to_half(grads[0].reshape(EXPERTS, D, FF))
        up_sum = weight_sums[1] + to_half(grads[1].reshape(EXPERTS, D, FF))
        down_sum = weight_sums[2] + to_half(grads[2].reshape(EXPERTS, FF, D))
        return (gate_sum, up_sum, down_sum), (act_sum.astype(jnp.bfloat16), prob_sum)

    zeros_in = (jnp.zeros((EXPERTS, D, FF), jnp.float32), jnp.zeros((EXPERTS, D, FF), jnp.float32), jnp.zeros((EXPERTS, FF, D), jnp.float32))
    weight_sums, outputs = lax.scan(one_group, zeros_in, inputs)
    grad_act = outputs[0].reshape(TOKENS, D)
    grad_prob = outputs[1].reshape(TOKENS, TOP)
    return (grad_act, grad_prob, weight_sums[0].astype(jnp.bfloat16), weight_sums[1].astype(jnp.bfloat16), weight_sums[2].astype(jnp.bfloat16))
```

```python
import functools

import jax
import jax.numpy as jnp
from jax import lax
from jax.experimental import pallas as pl
from jax.experimental.pallas import tpu as pltpu
from jax.sharding import PartitionSpec as P

TOP = 8
SRC = 128
CHUNK = 4
PEER = 48
LANES = 128
F32 = jnp.float32
BF16 = jnp.bfloat16

NT = (((1,), (1,)), ((), ()))
TN = (((0,), (0,)), ((), ()))


def dot(a, b, dims=(((1,), (0,)), ((), ()))):
    return lax.dot_general(a, b, dims, preferred_element_type=F32)


def expert_kernel(tgt, rel, dy, x, pr, wg, wu, wd, xs, gs, pa, dh, du, act, dxs, qs, ps):
    pairs = CHUNK // 2
    half = 2 * PEER

    def hot(pair):
        places = lax.broadcasted_iota(jnp.int32, (half, 2 * SRC), 0)
        return jnp.concatenate(
            [(places == tgt[0, e * pairs + pair, :][None, :]).astype(F32).astype(BF16) for e in range(2)], axis=0
        )

    for pair in range(pairs):
        rows = pl.ds(pair * 2 * SRC, 2 * SRC)
        spots = pl.ds(pair * half, half)
        pick = hot(pair)
        got_x = dot(pick, x[rows, :]).astype(BF16)
        got_g = dot(pick, dy[rows, :]).astype(BF16)
        local = rel[rows, :].astype(F32)
        probs = pr[rows, :].astype(F32)
        for e in range(2):
            part = slice(e * half, (e + 1) * half)
            xs[e, spots, :] = got_x[part]
            gs[e, spots, :] = got_g[part]
            mine = jnp.where(local == e, probs, 0.0).astype(BF16)
            col = jnp.sum(dot(pick[part], mine), axis=1, keepdims=True)
            ps[e, spots, :] = jnp.broadcast_to(col, (half, LANES))
    for e in range(2):
        h = dot(xs[e], wg[e])
        u = dot(xs[e], wu[e])
        dap = dot(gs[e], wd[e], NT)
        p = ps[e][:, :1]
        s = 1.0 / (1.0 + jnp.exp(-h))
        hs = h * s
        a = hs * u
        q = jnp.sum(a.astype(BF16).astype(F32) * dap, axis=1, keepdims=True)
        da = p * dap
        pa[e] = (p * a).astype(BF16)
        dh[e] = (da * u * s * (1.0 + h * (1.0 - s))).astype(BF16)
        du[e] = (da * hs).astype(BF16)
        dx = (dot(dh[e], wg[e], NT) + dot(du[e], wu[e], NT)).astype(BF16)
        wide = jnp.broadcast_to(q, (CHUNK * PEER, LANES)).astype(BF16)
        for pair in range(pairs):
            part = slice(pair * half, (pair + 1) * half)
            dxs[pair, pl.ds(e * half, half), :] = dx[part]
            qs[pair, pl.ds(e * half, half), :] = wide[part]
    for pair in range(pairs):
        rows = pl.ds(pair * 2 * SRC, 2 * SRC)
        pick = hot(pair)
        width = x.shape[1]
        act[rows, pl.ds(0, width)] = dot(pick, dxs[pair], TN).astype(BF16)
        local = rel[rows, :].astype(F32)
        ext = jnp.zeros(local.shape, F32)
        for e in range(2):
            part = slice(e * half, (e + 1) * half)
            ext = ext + jnp.where(local == e, dot(pick[part], qs[pair, pl.ds(e * half, half), :], TN), 0.0)
        act[rows, pl.ds(width, LANES)] = ext.astype(BF16)


def expert_pass(tgt, rel, whole, wg, wu, wd):
    rows, width = whole.shape[0], wg.shape[1]
    ff = wg.shape[2]
    n = rows // (SRC * CHUNK)
    span = CHUNK * SRC
    slots = CHUNK * PEER
    once = pl.Buffered(1)
    full = lambda shape: pl.BlockSpec(shape, lambda i: (0,) * len(shape), pipeline_mode=once)
    slot_spec = lambda w: pl.BlockSpec((2, slots, w), lambda i: (0, i, 0))
    slot_out = lambda w: jax.ShapeDtypeStruct((2, n * slots, w), BF16)
    return pl.pallas_call(
        expert_kernel,
        grid=(n,),
        in_specs=[
            pl.BlockSpec((1, CHUNK, 2 * SRC), lambda i: (i, 0, 0)),
            pl.BlockSpec((span, LANES), lambda i: (i, 0)),
            pl.BlockSpec((span, width), lambda i: (i, 0)),
            pl.BlockSpec((span, width), lambda i: (i, 1)),
            pl.BlockSpec((span, LANES), lambda i: (i, 2 * width // LANES)),
            full(wg.shape),
            full(wu.shape),
            full(wd.shape),
        ],
        out_specs=[
            slot_spec(width),
            slot_spec(width),
            slot_spec(ff),
            slot_spec(ff),
            slot_spec(ff),
            pl.BlockSpec((span, width + LANES), lambda i: (i, 0)),
        ],
        out_shape=[
            slot_out(width),
            slot_out(width),
            slot_out(ff),
            slot_out(ff),
            slot_out(ff),
            jax.ShapeDtypeStruct((rows, width + LANES), BF16),
        ],
        scratch_shapes=[
            pltpu.VMEM((CHUNK // 2, 4 * PEER, width), BF16),
            pltpu.VMEM((CHUNK // 2, 4 * PEER, LANES), BF16),
            pltpu.VMEM((2, slots, LANES), F32),
        ],
        compiler_params=pltpu.CompilerParams(vmem_limit_bytes=58 << 20),
        cost_estimate=pl.CostEstimate(flops=24 << 30, bytes_accessed=60 << 20, transcendentals=1 << 20),
        name="experts",
    )(tgt, rel, whole, whole, whole, wg, wu, wd)


def place_chunks(where, total, outs, step):
    my_x, my_c = where[0], where[1]
    for ahead in range(4):
        for own in range(2):
            core = my_c if own else 1 - my_c
            piece = lax.rem(my_x + ahead, 4) * 2 + core
            start = pl.multiple_of(piece * step, step)
            outs[own][ahead, 0] = total[pl.ds(start, step), :].astype(BF16)


def down_kernel(where, pa, gs, other, own, total):
    total[...] = dot(pa[0], gs[0], TN)
    place_chunks(where, total, (other, own), total.shape[0] // 8)


def up_kernel(where, xs, dh, du, other, own, total):
    ff = dh.shape[2]
    total[:, pl.ds(0, ff)] = dot(xs[0], dh[0], TN)
    total[:, pl.ds(ff, ff)] = dot(xs[0], du[0], TN)
    place_chunks(where, total, (other, own), total.shape[0] // 8)


def weight_pass(body, where, args, rows, cols, name):
    slots = args[0].shape[1]
    step = rows // 8
    out = jax.ShapeDtypeStruct((4, 2, step, cols), BF16)
    out_spec = pl.BlockSpec((4, 1, step, cols), lambda e: (0, e, 0, 0))
    return pl.pallas_call(
        body,
        grid=(2,),
        in_specs=[pl.BlockSpec(memory_space=pltpu.SMEM)]
        + [pl.BlockSpec((1, slots, a.shape[2]), lambda e: (e, 0, 0)) for a in args],
        out_specs=[out_spec, out_spec],
        out_shape=[out, out],
        scratch_shapes=[pltpu.VMEM((rows, cols), F32)],
        compiler_params=pltpu.CompilerParams(vmem_limit_bytes=58 << 20),
        cost_estimate=pl.CostEstimate(flops=4 * slots * rows * cols, bytes_accessed=16 << 20, transcendentals=0),
        name=name,
    )(where, *args)


def over_dp(other, own):
    swap = [(x * 2 + c, x * 2 + 1 - c) for x in range(4) for c in range(2)]
    right = [(x * 2 + c, (x + 1) % 4 * 2 + c) for x in range(4) for c in range(2)]
    left = [(x * 2 + c, (x + 3) % 4 * 2 + c) for x in range(4) for c in range(2)]
    got = lax.ppermute(other, "dp", swap)
    both = lambda i, e: own[i, e].astype(F32) + got[i, e].astype(F32)
    far_r = lax.ppermute(both(2, 0).astype(BF16), "dp", right)
    far_l = lax.ppermute(both(2, 1).astype(BF16), "dp", left)
    near_r = jnp.stack([both(1, 0) + far_r.astype(F32), both(1, 1)]).astype(BF16)
    near_l = jnp.stack([both(3, 0), both(3, 1) + far_l.astype(F32)]).astype(BF16)
    near_r = lax.ppermute(near_r, "dp", right)
    near_l = lax.ppermute(near_l, "dp", left)
    return own[0].astype(F32) + got[0].astype(F32) + near_r.astype(F32) + near_l.astype(F32)


def tables(ids, first):
    rows = ids.shape[0]
    mine = first + jnp.arange(2, dtype=jnp.int32)
    hit = jnp.any(ids[None] == mine[:, None, None], axis=2)
    hit = hit.reshape(2, rows // SRC, SRC)
    before = jnp.triu(jnp.ones((SRC, SRC), BF16), 1)
    rank = jnp.einsum("ebr,rs->ebs", hit.astype(BF16), before, preferred_element_type=F32).astype(jnp.int32)
    second = (jnp.arange(rows // SRC, dtype=jnp.int32) % 2 * PEER)[None, :, None]
    tgt = jnp.where(hit, rank + second, -1)
    tgt = tgt.reshape(2, rows // (SRC * CHUNK), CHUNK // 2, 2 * SRC)
    tgt = jnp.transpose(tgt, (1, 0, 2, 3)).reshape(rows // (SRC * CHUNK), CHUNK, 2 * SRC)
    rel = jnp.pad(ids - first, ((0, 0), (0, LANES - TOP)), constant_values=-1).astype(BF16)
    return tgt, rel


def on_device(activations, out_grad, gate_probs, expert_ids, w_gate, w_up, w_down):
    my_index = lax.axis_index("expert")
    dp_index = lax.axis_index("dp")
    width = activations.shape[1]
    ff = w_gate.shape[2]
    payload = jnp.concatenate(
        [out_grad, activations, jnp.pad(gate_probs, ((0, 0), (0, LANES - TOP)))], axis=1
    )
    whole = lax.all_gather(payload, "expert", axis=0, tiled=True)
    tgt, rel = tables(expert_ids, my_index * 2)
    xs, gs, pa, dh, du, act = expert_pass(tgt, rel, whole, w_gate, w_up, w_down)
    act_sum = lax.psum_scatter(act, "expert", scatter_dimension=0, tiled=True)
    where = jnp.stack([dp_index // 2, dp_index % 2]).astype(jnp.int32)
    down = weight_pass(down_kernel, where, (pa, gs), ff, width, "down_grad")
    up = weight_pass(up_kernel, where, (xs, dh, du), width, 2 * ff, "up_grad")
    grad_down = over_dp(*down)
    grad_both = over_dp(*up)
    return (
        act_sum[:, :width],
        act_sum[:, width : width + TOP].astype(F32),
        grad_both[:, :, :ff].astype(BF16),
        grad_both[:, :, ff:].astype(BF16),
        grad_down.astype(BF16),
    )


def solution(mesh):
    placed = (
        P(("dp", "expert"), None),
        P(("dp", "expert"), None),
        P(("dp", "expert"), None),
        P("dp", None),
        P("expert", None, None),
        P("expert", None, None),
        P("expert", None, None),
    )
    return jax.shard_map(
        on_device,
        mesh=mesh,
        in_specs=placed,
        out_specs=(
            P(("dp", "expert"), None),
            P(("dp", "expert"), None),
            P("expert", "dp", None),
            P("expert", "dp", None),
            P("expert", "dp", None),
        ),
        check_vma=False,
    )
```

```python
import functools

import jax
import jax.numpy as jnp
from jax import lax
from jax.experimental import pallas as pl
from jax.experimental.pallas import tpu as pltpu
from jax.sharding import PartitionSpec as P

TOP = 8
SRC = 128
CHUNK = 4
PEER = 48
LANES = 128
F32 = jnp.float32
BF16 = jnp.bfloat16

NT = (((1,), (1,)), ((), ()))
TN = (((0,), (0,)), ((), ()))


def dot(a, b, dims=(((1,), (0,)), ((), ()))):
    return lax.dot_general(a, b, dims, preferred_element_type=F32)
VMEM = 58 << 20


def hot(tgt, plane, pair):
    half = 2 * PEER
    places = lax.broadcasted_iota(jnp.int32, (half, 2 * SRC), 0)
    return jnp.concatenate(
        [(places == tgt[plane, e * 2 + pair, :][None, :]).astype(F32).astype(BF16) for e in range(2)], axis=0
    )


def stage_kernel(n, tgt_x, tgt_g, rel, *refs):
    x, g, (wg, wu, wd) = refs[: 2 * n], refs[2 * n : 4 * n], refs[4 * n : 4 * n + 3]
    xs, pa, ab, wp, hp, gs, dap, probs_of, picked = refs[-9:]
    half = 2 * PEER
    slots = CHUNK * PEER
    width, ff = wg.shape[1], wg.shape[2]

    @pl.when(pl.program_id(0) == 0)
    def _():
        for plane in range(n):
            for pair in range(2):
                spots = pl.ds(pair * half, half)
                pick = hot(tgt_x, plane, pair)
                rows = x[plane * 2 + pair]
                got = dot(pick, rows[:, pl.ds(0, width)]).astype(BF16)
                local = rel[plane, pl.ds(pair * 2 * SRC, 2 * SRC), :].astype(F32)
                probs = rows[:, pl.ds(width, LANES)].astype(F32)
                got_g = dot(hot(tgt_g, plane, pair), g[plane * 2 + pair][...]).astype(BF16)
                for e in range(2):
                    part = slice(e * half, (e + 1) * half)
                    xs[e, plane, spots, :] = got[part]
                    picked[e, pl.ds(plane * slots + pair * half, half), :] = got_g[part]
                    for i in range(2):
                        at = e * half + i * PEER
                        gs[e, pair * 2 + i, plane] = got_g[at : at + PEER]
                    mine = jnp.where(local == e, probs, 0.0).astype(BF16)
                    col = jnp.sum(dot(pick[part], mine), axis=1, keepdims=True)
                    probs_of[e, pl.ds(plane * slots + pair * half, half), :] = jnp.broadcast_to(col, (half, LANES))

    e = pl.program_id(0)
    rows = xs[e].reshape(n * slots, width)
    h = dot(rows, wg[0])
    u = dot(rows, wu[0])
    p = probs_of[e][:, :1]
    s = 1.0 / (1.0 + jnp.exp(-h))
    hs = h * s
    a = hs * u
    shape = (n, slots, ff)
    ab[0] = a.astype(BF16).reshape(shape)
    pa[0] = (p * a).astype(BF16).reshape(shape)
    wp[0] = (p * (u * s * (1.0 + h * (1.0 - s)))).reshape(shape)
    hp[0] = (p * hs).reshape(shape)
    back = dot(picked[e], wd[0], NT)
    for plane in range(n):
        for i in range(CHUNK):
            at = plane * slots + i * PEER
            dap[0, i, plane] = back[at : at + PEER]


def fixed(shape, *at):
    return pl.BlockSpec(shape, lambda e: at, pipeline_mode=pl.Buffered(1))


def by_expert(shape, *at):
    return pl.BlockSpec((1, *shape), lambda e: (e, *at))


def stage_pass(n, at, tables, x, g, weights, prior):
    wg, wu, wd = weights
    width, ff = wg.shape[1], wg.shape[2]
    slots = CHUNK * PEER
    by_plane = [(width, BF16), (ff, BF16), (ff, BF16), (ff, F32), (ff, F32)]
    by_line = [(width, BF16), (ff, F32)]
    held = [] if prior is None else list(prior)
    before = 3 + len(x) + len(g) + 3
    return pl.pallas_call(
        functools.partial(stage_kernel, n),
        grid=(2,),
        in_specs=[fixed((n, CHUNK, 2 * SRC), at, 0, 0)] * 2
        + [fixed((n, CHUNK * SRC, LANES), at, 0, 0)]
        + [fixed(v.shape, 0, 0) for v in (*x, *g)]
        + [by_expert(w.shape[1:], 0, 0) for w in weights]
        + [pl.BlockSpec(memory_space=pl.ANY)] * len(held),
        out_specs=[fixed((2, n, slots, width), 0, at, 0, 0)]
        + [by_expert((n, slots, ff), at, 0, 0)] * 4
        + [fixed((2, 4, n, PEER, width), 0, 0, at, 0, 0), by_expert((4, n, PEER, ff), 0, at, 0, 0)],
        out_shape=[jax.ShapeDtypeStruct((2, 4, slots, w), t) for w, t in by_plane]
        + [jax.ShapeDtypeStruct((2, 4, 4, PEER, w), t) for w, t in by_line],
        scratch_shapes=[pltpu.VMEM((2, n * slots, LANES), F32), pltpu.VMEM((2, n * slots, width), BF16)],
        input_output_aliases={before + i: i for i in range(len(held))},
        compiler_params=pltpu.CompilerParams(vmem_limit_bytes=VMEM),
        cost_estimate=pl.CostEstimate(flops=1 << 28, bytes_accessed=1 << 19, transcendentals=0),
        name="stage",
    )(*tables, *x, *g, *weights, *held)


def turn_kernel(wg, wu, out):
    ff = wg.shape[2]
    out[0, pl.ds(0, ff), :] = wg[0].T
    out[0, pl.ds(ff, ff), :] = wu[0].T


def turn_pass(wg, wu):
    width, ff = wg.shape[1], wg.shape[2]
    return pl.pallas_call(
        turn_kernel,
        grid=(2,),
        in_specs=[by_expert((width, ff), 0, 0)] * 2,
        out_specs=by_expert((2 * ff, width), 0, 0),
        out_shape=jax.ShapeDtypeStruct((2, 2 * ff, width), BF16),
        compiler_params=pltpu.CompilerParams(vmem_limit_bytes=VMEM),
        cost_estimate=pl.CostEstimate(flops=1 << 28, bytes_accessed=1 << 19, transcendentals=0),
        name="turn",
    )(wg, wu)


def back_kernel(place, tgt, rel, ab, wp, hp, dap, wt_hbm, dhu, act, wt, dxs, qs, sem):
    half = 2 * PEER
    slots = 2 * CHUNK * PEER
    width = wt.shape[2]
    ff = ab.shape[3]
    step = pl.program_id(0)
    first = step == 0

    @pl.when(first)
    def _():
        for e in range(2):
            pltpu.make_async_copy(wt_hbm.at[e], wt.at[e], sem.at[e]).start()

    for e in range(2):
        back = dap[e].reshape(slots, ff)
        q = jnp.sum(ab[e].reshape(slots, ff).astype(F32) * back, axis=1, keepdims=True)
        dhu[e, :, pl.ds(0, ff)] = (back * wp[e].reshape(slots, ff)).astype(BF16)
        dhu[e, :, pl.ds(ff, ff)] = (back * hp[e].reshape(slots, ff)).astype(BF16)
        wide = jnp.broadcast_to(q, (slots, LANES)).astype(BF16)
        for pair in range(4):
            qs[pair, pl.ds(e * half, half), :] = wide[pair * half : (pair + 1) * half]
    for e in range(2):

        @pl.when(first)
        def _():
            pltpu.make_async_copy(wt_hbm.at[e], wt.at[e], sem.at[e]).wait()

        dx = dot(dhu[e], wt[e]).astype(BF16)
        for pair in range(4):
            dxs[pair, pl.ds(e * half, half), :] = dx[pair * half : (pair + 1) * half]
    for plane in range(2):
        high = place[2 + step * 2 + plane]
        for pair in range(2):
            held = plane * 2 + pair
            pick = hot(tgt, plane, pair)
            rows = dot(pick, dxs[held], TN).astype(BF16)
            local = rel[plane, pl.ds(pair * 2 * SRC, 2 * SRC), :].astype(F32)
            ext = jnp.zeros(local.shape, F32)
            for e in range(2):
                part = slice(e * half, (e + 1) * half)
                ext = ext + jnp.where(local == e, dot(pick[part], qs[held, pl.ds(e * half, half), :], TN), 0.0)
            ext = ext.astype(BF16)
            for i in range(2):
                part = slice(i * SRC, (i + 1) * SRC)
                y = place[6 + pair * 2 + i]
                act[high, 0, y, :, pl.ds(0, width)] = rows[part]
                act[high, 0, y, :, pl.ds(width, LANES)] = ext[part]


def back_pass(place, tgt, rel, ab, wp, hp, dap, wt):
    width, ff = wt.shape[2], ab.shape[3]
    slots = CHUNK * PEER
    by_plane = pl.BlockSpec((2, 2, slots, ff), lambda i, at: (0, i, 0, 0))
    return pl.pallas_call(
        back_kernel,
        grid_spec=pltpu.PrefetchScalarGridSpec(
            num_scalar_prefetch=1,
            grid=(2,),
            in_specs=[
                pl.BlockSpec((2, CHUNK, 2 * SRC), lambda i, at: (i, 0, 0)),
                pl.BlockSpec((2, CHUNK * SRC, LANES), lambda i, at: (i, 0, 0)),
                by_plane,
                by_plane,
                by_plane,
                pl.BlockSpec((2, 2, 4, PEER, ff), lambda i, at: (0, i, 0, 0, 0)),
                pl.BlockSpec(memory_space=pl.ANY),
            ],
            out_specs=[
                pl.BlockSpec((2, 2 * slots, 2 * ff), lambda i, at: (0, i, 0)),
                pl.BlockSpec((2, 1, 4, SRC, width + LANES), lambda i, at: (0, at[i], 0, 0, 0)),
            ],
            scratch_shapes=[
                pltpu.VMEM(wt.shape, BF16),
                pltpu.VMEM((4, 4 * PEER, width), BF16),
                pltpu.VMEM((4, 4 * PEER, LANES), BF16),
                pltpu.SemaphoreType.DMA((2,)),
            ],
        ),
        out_shape=[
            jax.ShapeDtypeStruct((2, 4 * slots, 2 * ff), BF16),
            jax.ShapeDtypeStruct((2, 2, 4, SRC, width + LANES), BF16),
        ],
        compiler_params=pltpu.CompilerParams(vmem_limit_bytes=VMEM),
        cost_estimate=pl.CostEstimate(flops=14 << 30, bytes_accessed=32 << 20, transcendentals=0),
        name="back",
    )(place, tgt, rel, ab, wp, hp, dap, wt)


def place_chunks(where, total, outs, step):
    my_x, my_c = where[0], where[1]
    for ahead in range(4):
        for own in range(2):
            core = my_c if own else 1 - my_c
            piece = lax.rem(my_x + ahead, 4) * 2 + core
            start = pl.multiple_of(piece * step, step)
            outs[own][ahead, 0] = total[pl.ds(start, step), :].astype(BF16)


def down_kernel(where, pa, gs, other, own, total):
    total[...] = dot(pa[0], gs[0], TN)
    place_chunks(where, total, (other, own), total.shape[0] // 8)


def up_kernel(where, xs, dhu, other, own, total):
    total[...] = dot(xs[0], dhu[0], TN)
    place_chunks(where, total, (other, own), total.shape[0] // 8)


def weight_pass(body, where, args, rows, cols, name):
    slots = args[0].shape[1]
    step = rows // 8
    out = jax.ShapeDtypeStruct((4, 2, step, cols), BF16)
    out_spec = pl.BlockSpec((4, 1, step, cols), lambda e: (0, e, 0, 0))
    return pl.pallas_call(
        body,
        grid=(2,),
        in_specs=[pl.BlockSpec(memory_space=pltpu.SMEM)]
        + [pl.BlockSpec((1, slots, a.shape[2]), lambda e: (e, 0, 0)) for a in args],
        out_specs=[out_spec, out_spec],
        out_shape=[out, out],
        scratch_shapes=[pltpu.VMEM((rows, cols), F32)],
        compiler_params=pltpu.CompilerParams(vmem_limit_bytes=VMEM),
        cost_estimate=pl.CostEstimate(flops=4 * slots * rows * cols, bytes_accessed=16 << 20, transcendentals=0),
        name=name,
    )(where, *args)


def along_x(by):
    return [(x * 2 + c, (x + by) % 4 * 2 + c) for x in range(4) for c in range(2)]


def swap_cores(other):
    return lax.ppermute(other, "dp", [(x * 2 + c, x * 2 + 1 - c) for x in range(4) for c in range(2)])


def both(own, got, *at):
    return own[at].astype(F32) + got[at].astype(F32)


def send_far(own, got):
    return (
        lax.ppermute(both(own, got, 2, 0).astype(BF16), "dp", along_x(1)),
        lax.ppermute(both(own, got, 2, 1).astype(BF16), "dp", along_x(-1)),
    )


def send_near(own, got, far):
    ahead = jnp.stack([both(own, got, 1, 0) + far[0].astype(F32), both(own, got, 1, 1)]).astype(BF16)
    back = jnp.stack([both(own, got, 3, 0), both(own, got, 3, 1) + far[1].astype(F32)]).astype(BF16)
    ahead, back = lax.ppermute(ahead, "dp", along_x(1)), lax.ppermute(back, "dp", along_x(-1))
    return both(own, got, 0) + ahead.astype(F32) + back.astype(F32)


def along_y(by):
    return [(z * 4 + y, z * 4 + (y + by) % 4) for z in range(4) for y in range(4)]


def along_z(by):
    return [(z * 4 + y, (z + by) % 4 * 4 + y) for z in range(4) for y in range(4)]


def send(value, route):
    return lax.ppermute(value, "expert", route)


def gather_line(block, ring):
    half = block.shape[0] // 2
    back, ahead = send(block, ring(1)), send(block, ring(-1))
    far = [send(back[:half], ring(1)), send(ahead[half:], ring(-1))]
    return jnp.concatenate([block, *far], axis=0), jnp.concatenate([back, ahead], axis=0)


def tables(ids, first, my_z, my_y):
    mine = first + jnp.arange(2, dtype=jnp.int32)
    ids = ids.reshape(4, 4, SRC, TOP)
    ids = jnp.roll(ids, (-my_z, -my_y), (0, 1))
    ids = jnp.stack([ids[0], ids[2], ids[3], ids[1]])
    ids = jnp.stack([ids[:, 0], ids[:, 2], ids[:, 3], ids[:, 1]], axis=1)
    hit = jnp.any(ids[None] == mine[:, None, None, None, None], axis=4)
    before = jnp.triu(jnp.ones((SRC, SRC), BF16), 1)
    rank = jnp.einsum("ezyr,rs->ezys", hit.astype(BF16), before, preferred_element_type=F32).astype(jnp.int32)
    slot = jnp.where(hit, rank, -2 * PEER)

    def by_pairs(t):
        t = t.reshape(2, 4, 2, 2, SRC) + jnp.arange(2, dtype=jnp.int32)[:, None] * PEER
        return jnp.transpose(t, (1, 0, 2, 3, 4)).reshape(4, CHUNK, 2 * SRC)

    rel = jnp.pad((ids - first).reshape(4, 4 * SRC, TOP), ((0, 0), (0, 0), (0, LANES - TOP)), constant_values=-1)
    return by_pairs(slot), by_pairs(jnp.swapaxes(slot, 1, 2)), rel.astype(BF16)


def on_device(activations, out_grad, gate_probs, expert_ids, w_gate, w_up, w_down):
    my_index = lax.axis_index("expert")
    dp_index = lax.axis_index("dp")
    width = activations.shape[1]
    ff = w_gate.shape[2]
    my_z, my_y = my_index // 4, my_index % 4
    rows = jnp.concatenate([activations, jnp.pad(gate_probs, ((0, 0), (0, LANES - TOP)))], axis=1)
    tgt_x, tgt_g, rel = tables(expert_ids, my_index * 2, my_z, my_y)
    weights = (w_gate, w_up, w_down)
    x_own, g_own = lax.optimization_barrier((gather_line(rows, along_y), gather_line(out_grad, along_z)))
    (x_lo, x_hi), (g_lo, g_hi) = x_own, g_own
    onward = (
        send(x_hi, along_z(1)),
        send(x_lo, along_z(-1)),
        send(g_hi, along_y(1)),
        send(g_lo, along_y(-1)),
    )
    turned = turn_pass(w_gate, w_up)
    made = stage_pass(1, 0, (tgt_x, tgt_g, rel), x_own, g_own, weights, None)
    x_lo, x_hi, g_lo, g_hi, onward, turned, made = lax.optimization_barrier(
        (x_lo, x_hi, g_lo, g_hi, onward, turned, made)
    )
    x_near = send(x_lo, along_z(1)), onward[0], onward[1], send(x_hi, along_z(-1))
    g_near = send(g_lo, along_y(1)), onward[2], onward[3], send(g_hi, along_y(-1))
    x_far = send(onward[1], along_z(-1)), send(onward[0], along_z(1))
    g_far = send(onward[3], along_y(-1)), send(onward[2], along_y(1))
    made = stage_pass(2, 1, (tgt_x, tgt_g, rel), x_near, g_near, weights, made)
    made = stage_pass(1, 1, (tgt_x, tgt_g, rel), x_far, g_far, weights, made)
    xs, pa, ab, wp, hp, gs, dap = made
    away = jnp.array([0, 2, 3, 1], jnp.int32)
    plane_z = (my_z + away) % 4
    place = jnp.concatenate([plane_z[::2] % 2, plane_z // 2, (my_y + away) % 4]).astype(jnp.int32)
    dhu, act = back_pass(place, tgt_x, rel, ab, wp, hp, dap, turned)
    act_sum = lax.psum_scatter(act.reshape(16 * SRC, -1), "expert", scatter_dimension=0, tiled=True)
    where = jnp.stack([dp_index // 2, dp_index % 2]).astype(jnp.int32)
    flat = lambda v: v.reshape(2, 16 * PEER, -1)
    up = weight_pass(up_kernel, where, (flat(xs), dhu), width, 2 * ff, "up_grad")
    down = weight_pass(down_kernel, where, (flat(pa), flat(gs)), ff, width, "down_grad")
    got_up, got_down = swap_cores(up[0]), swap_cores(down[0])
    far_up = send_far(up[1], got_up)
    got_down, far_up = lax.optimization_barrier((got_down, far_up))
    far_down = send_far(down[1], got_down)
    grad_both = send_near(up[1], got_up, far_up)
    grad_down = send_near(down[1], got_down, far_down)
    return (
        act_sum[:, :width],
        act_sum[:, width : width + TOP].astype(F32),
        grad_both[:, :, :ff].astype(BF16),
        grad_both[:, :, ff:].astype(BF16),
        grad_down.astype(BF16),
    )


def solution(mesh):
    placed = (
        P(("dp", "expert"), None),
        P(("dp", "expert"), None),
        P(("dp", "expert"), None),
        P("dp", None),
        P("expert", None, None),
        P("expert", None, None),
        P("expert", None, None),
    )
    return jax.shard_map(
        on_device,
        mesh=mesh,
        in_specs=placed,
        out_specs=(
            P(("dp", "expert"), None),
            P(("dp", "expert"), None),
            P("expert", "dp", None),
            P("expert", "dp", None),
            P("expert", "dp", None),
        ),
        check_vma=False,
    )
```

```python
import functools

import jax
import jax.numpy as jnp
from jax import lax
from jax.experimental import pallas as pl
from jax.experimental.pallas import tpu as pltpu
from jax.sharding import PartitionSpec as P

TOP = 8
SRC = 128
CHUNK = 4
PEER = 48
LANES = 128
F32 = jnp.float32
BF16 = jnp.bfloat16

NT = (((1,), (1,)), ((), ()))
TN = (((0,), (0,)), ((), ()))


def dot(a, b, dims=(((1,), (0,)), ((), ()))):
    return lax.dot_general(a, b, dims, preferred_element_type=F32)
VMEM = 58 << 20


def hot(tgt, plane, pair):
    half = 2 * PEER
    places = lax.broadcasted_iota(jnp.int32, (half, 2 * SRC), 0)
    return jnp.concatenate(
        [(places == tgt[plane, e * 2 + pair, :][None, :]).astype(F32).astype(BF16) for e in range(2)], axis=0
    )


def pick_rows(n, tgt_x, tgt_g, rel, x, g, xs, gs, probs_of, picked):
    half = 2 * PEER
    slots = CHUNK * PEER
    width = xs.shape[3]
    for plane in range(n):
        for pair in range(2):
            spots = pl.ds(pair * half, half)
            pick = hot(tgt_x, plane, pair)
            rows = x[plane * 2 + pair]
            got = dot(pick, rows[:, pl.ds(0, width)]).astype(BF16)
            local = rel[plane, pl.ds(pair * 2 * SRC, 2 * SRC), :].astype(F32)
            probs = rows[:, pl.ds(width, LANES)].astype(F32)
            got_g = dot(hot(tgt_g, plane, pair), g[plane * 2 + pair][...]).astype(BF16)
            for e in range(2):
                part = slice(e * half, (e + 1) * half)
                xs[e, plane, spots, :] = got[part]
                picked[e, pl.ds(plane * slots + pair * half, half), :] = got_g[part]
                for i in range(2):
                    at = e * half + i * PEER
                    gs[e, pair * 2 + i, plane] = got_g[at : at + PEER]
                mine = jnp.where(local == e, probs, 0.0).astype(BF16)
                col = jnp.sum(dot(pick[part], mine), axis=1, keepdims=True)
                probs_of[e, pl.ds(plane * slots + pair * half, half), :] = jnp.broadcast_to(col, (half, LANES))


def products(rows, picked, p, wg, wu, wd):
    h = dot(rows, wg)
    u = dot(rows, wu)
    s = 1.0 / (1.0 + jnp.exp(-h))
    hs = h * s
    a = hs * u
    wp = p * (u * s * (1.0 + h * (1.0 - s)))
    return tuple(v.astype(BF16) for v in (p * a, a, wp, p * hs, dot(picked, wd, NT)))


def stage_kernel(n, tgt_x, tgt_g, rel, *refs):
    x, g, (wg, wu, wd) = refs[: 2 * n], refs[2 * n : 4 * n], refs[4 * n : 4 * n + 3]
    xs, pa, ab, wp, hp, gs, dap, probs_of, picked = refs[-9:]
    slots = CHUNK * PEER
    width, ff = wg.shape[1], wg.shape[2]
    e = pl.program_id(0)

    @pl.when(e == 0)
    def _():
        pick_rows(n, tgt_x, tgt_g, rel, x, g, xs, gs, probs_of, picked)

    rows = xs[e].reshape(n * slots, width)
    *made, back = products(rows, picked[e], probs_of[e][:, :1], wg[0], wu[0], wd[0])
    for out, value in zip((pa, ab, wp, hp), made):
        out[0] = value.reshape(n, slots, ff)
    for plane in range(n):
        for i in range(CHUNK):
            at = plane * slots + i * PEER
            dap[0, i, plane] = back[at : at + PEER]


def fixed(shape, *at):
    return pl.BlockSpec(shape, lambda e: at, pipeline_mode=pl.Buffered(1))


def by_expert(shape, *at):
    return pl.BlockSpec((1, *shape), lambda e: (e, *at))


def stage_pass(n, at, tables, x, g, weights, prior):
    wg, wu, wd = weights
    width, ff = wg.shape[1], wg.shape[2]
    slots = CHUNK * PEER
    by_plane = [width, ff, ff, ff, ff]
    by_line = [width, ff]
    held = [] if prior is None else list(prior)
    before = 3 + len(x) + len(g) + 3
    return pl.pallas_call(
        functools.partial(stage_kernel, n),
        grid=(2,),
        in_specs=[fixed((n, CHUNK, 2 * SRC), at, 0, 0)] * 2
        + [fixed((n, CHUNK * SRC, LANES), at, 0, 0)]
        + [fixed(v.shape, 0, 0) for v in (*x, *g)]
        + [by_expert(w.shape[1:], 0, 0) for w in weights]
        + [pl.BlockSpec(memory_space=pl.ANY)] * len(held),
        out_specs=[fixed((2, n, slots, width), 0, at, 0, 0)]
        + [by_expert((n, slots, ff), at, 0, 0)] * 4
        + [fixed((2, 4, n, PEER, width), 0, 0, at, 0, 0), by_expert((4, n, PEER, ff), 0, at, 0, 0)],
        out_shape=[jax.ShapeDtypeStruct((2, 4, slots, w), BF16) for w in by_plane]
        + [jax.ShapeDtypeStruct((2, 4, 4, PEER, w), BF16) for w in by_line],
        scratch_shapes=[pltpu.VMEM((2, n * slots, LANES), F32), pltpu.VMEM((2, n * slots, width), BF16)],
        input_output_aliases={before + i: i for i in range(len(held))},
        compiler_params=pltpu.CompilerParams(vmem_limit_bytes=VMEM),
        cost_estimate=pl.CostEstimate(flops=1 << 28, bytes_accessed=1 << 19, transcendentals=0),
        name="stage",
    )(*tables, *x, *g, *weights, *held)


def turn_kernel(wg, wu, out):
    ff = wg.shape[2]
    out[0, pl.ds(0, ff), :] = wg[0].T
    out[0, pl.ds(ff, ff), :] = wu[0].T


def turn_pass(wg, wu):
    width, ff = wg.shape[1], wg.shape[2]
    return pl.pallas_call(
        turn_kernel,
        grid=(2,),
        in_specs=[by_expert((width, ff), 0, 0)] * 2,
        out_specs=by_expert((2 * ff, width), 0, 0),
        out_shape=jax.ShapeDtypeStruct((2, 2 * ff, width), BF16),
        compiler_params=pltpu.CompilerParams(vmem_limit_bytes=VMEM),
        cost_estimate=pl.CostEstimate(flops=1 << 28, bytes_accessed=1 << 19, transcendentals=0),
        name="turn",
    )(wg, wu)


def held_copies(held, kept, wt_hbm, wt, sem):
    copies = [(wt_hbm.at[e], wt.at[e]) for e in range(2)]
    for i, (src, dst) in enumerate(zip(held, kept)):
        for part in (pl.ds(0, 1), pl.ds(2, 2)):
            at = (slice(None), slice(None), part) if i == 3 else (slice(None), part)
            copies.append((src.at[at], dst.at[at]))
    return [pltpu.make_async_copy(src, dst, sem.at[i]) for i, (src, dst) in enumerate(copies)]


def tail_kernel(place, tgt_x, tgt_g, rel_x, tgt, rel, x_lo, x_hi, g_lo, g_hi, wg, wu, wd, wt_hbm, *refs):
    held = refs[3:7]
    xs, pa, gs, dhu, act, wt, ab, wp, hp, dap, probs_of, picked, dxs, qs, sem = refs[7:]
    kept = (ab, wp, hp, dap)
    half = 2 * PEER
    slots = CHUNK * PEER
    width, ff = wg.shape[1], wg.shape[2]
    step = pl.program_id(0)

    @pl.when(step == 0)
    def _():
        for copy in held_copies(held, kept, wt_hbm, wt, sem):
            copy.start()
        pick_rows(1, tgt_x, tgt_g, rel_x, (x_lo, x_hi), (g_lo, g_hi), xs, gs, probs_of, picked)

    @pl.when(step < 2)
    def _():
        made = products(xs[step, 0], picked[step], probs_of[step][:, :1], wg[0], wu[0], wd[0])
        pa[0, 0] = made[0]
        for out, value in zip((ab, wp, hp), made[1:4]):
            out[step, 1] = value
        for i in range(CHUNK):
            dap[step, i, 1] = made[4][i * PEER : (i + 1) * PEER]

    @pl.when(step == 2)
    def _():
        for copy in held_copies(held, kept, wt_hbm, wt, sem):
            copy.wait()

    @pl.when(step >= 2)
    def _():
        k = step - 2
        for e in range(2):
            back = dap[e, k].astype(F32).reshape(slots, ff)
            q = jnp.sum(ab[e, k].astype(F32) * back, axis=1, keepdims=True)
            dhu[e, :, pl.ds(0, ff)] = (back * wp[e, k].astype(F32)).astype(BF16)
            dhu[e, :, pl.ds(ff, ff)] = (back * hp[e, k].astype(F32)).astype(BF16)
            wide = jnp.broadcast_to(q, (slots, LANES)).astype(BF16)
            for pair in range(2):
                qs[pair, pl.ds(e * half, half), :] = wide[pair * half : (pair + 1) * half]
        for e in range(2):
            dx = dot(dhu[e], wt[e]).astype(BF16)
            for pair in range(2):
                dxs[pair, pl.ds(e * half, half), :] = dx[pair * half : (pair + 1) * half]
        for pair in range(2):
            pick = hot(tgt, 0, pair)
            rows = dot(pick, dxs[pair], TN).astype(BF16)
            local = rel[0, pl.ds(pair * 2 * SRC, 2 * SRC), :].astype(F32)
            ext = jnp.zeros(local.shape, F32)
            for e in range(2):
                part = slice(e * half, (e + 1) * half)
                ext = ext + jnp.where(local == e, dot(pick[part], qs[pair, pl.ds(e * half, half), :], TN), 0.0)
            ext = ext.astype(BF16)
            for i in range(2):
                part = slice(i * SRC, (i + 1) * SRC)
                y = place[4 + pair * 2 + i]
                act[0, y, :, pl.ds(0, width)] = rows[part]
                act[0, y, :, pl.ds(width, LANES)] = ext[part]


def tail_pass(place, tables, x, g, weights, wt, made):
    tgt_x, tgt_g, rel = tables
    wg, wu, wd = weights
    width, ff = wg.shape[1], wg.shape[2]
    slots = CHUNK * PEER
    xs, pa, ab, wp, hp, gs, dap = made
    once = pl.Buffered(1)
    kept = lambda shape, *at: pl.BlockSpec(shape, lambda i, p: at, pipeline_mode=once)
    plane = lambda i: jnp.maximum(i - 2, 0)
    expert = lambda i: jnp.minimum(i, 1)
    of_plane = lambda *shape: pl.BlockSpec((1, *shape), lambda i, p: (plane(i), 0, 0))
    of_expert = lambda w: pl.BlockSpec((1, *w.shape[1:]), lambda i, p: (expert(i), 0, 0))
    anywhere = pl.BlockSpec(memory_space=pl.ANY)
    return pl.pallas_call(
        tail_kernel,
        grid_spec=pltpu.PrefetchScalarGridSpec(
            num_scalar_prefetch=1,
            grid=(6,),
            in_specs=[
                kept((1, CHUNK, 2 * SRC), 1, 0, 0),
                kept((1, CHUNK, 2 * SRC), 1, 0, 0),
                kept((1, CHUNK * SRC, LANES), 1, 0, 0),
                of_plane(CHUNK, 2 * SRC),
                of_plane(CHUNK * SRC, LANES),
            ]
            + [kept(v.shape, 0, 0) for v in (*x, *g)]
            + [of_expert(w) for w in weights]
            + [anywhere] * 8,
            out_specs=[
                kept((2, 1, slots, width), 0, 1, 0, 0),
                pl.BlockSpec((1, 1, slots, ff), lambda i, p: (expert(i), 1, 0, 0)),
                kept((2, 4, 1, PEER, width), 0, 0, 1, 0, 0),
                pl.BlockSpec((2, slots, 2 * ff), lambda i, p: (0, plane(i), 0)),
                pl.BlockSpec((1, 4, SRC, width + LANES), lambda i, p: (p[plane(i)], 0, 0, 0)),
            ],
            scratch_shapes=[
                pltpu.VMEM(wt.shape, BF16),
                pltpu.VMEM(ab.shape, BF16),
                pltpu.VMEM(wp.shape, BF16),
                pltpu.VMEM(hp.shape, BF16),
                pltpu.VMEM(dap.shape, BF16),
                pltpu.VMEM((2, slots, LANES), F32),
                pltpu.VMEM((2, slots, width), BF16),
                pltpu.VMEM((2, 4 * PEER, width), BF16),
                pltpu.VMEM((2, 4 * PEER, LANES), BF16),
                pltpu.SemaphoreType.DMA((10,)),
            ],
        ),
        out_shape=[jax.ShapeDtypeStruct(v.shape, BF16) for v in (xs, pa, gs)]
        + [
            jax.ShapeDtypeStruct((2, 4 * slots, 2 * ff), BF16),
            jax.ShapeDtypeStruct((4, 4, SRC, width + LANES), BF16),
        ],
        input_output_aliases={14: 0, 15: 1, 16: 2},
        compiler_params=pltpu.CompilerParams(vmem_limit_bytes=VMEM),
        cost_estimate=pl.CostEstimate(flops=14 << 30, bytes_accessed=32 << 20, transcendentals=0),
        name="tail",
    )(place, tgt_x, tgt_g, rel, tgt_x, rel, *x, *g, wg, wu, wd, wt, xs, pa, gs, ab, wp, hp, dap)


def place_chunks(where, total, outs, step):
    my_x, my_c = where[0], where[1]
    for ahead in range(4):
        for own in range(2):
            core = my_c if own else 1 - my_c
            piece = lax.rem(my_x + ahead, 4) * 2 + core
            start = pl.multiple_of(piece * step, step)
            outs[own][ahead, 0] = total[pl.ds(start, step), :].astype(BF16)


def down_kernel(where, pa, gs, other, own, total):
    total[...] = dot(pa[0], gs[0], TN)
    place_chunks(where, total, (other, own), total.shape[0] // 8)


def up_kernel(where, xs, dhu, other, own, total):
    total[...] = dot(xs[0], dhu[0], TN)
    place_chunks(where, total, (other, own), total.shape[0] // 8)


def weight_pass(body, where, args, rows, cols, name):
    slots = args[0].shape[1]
    step = rows // 8
    out = jax.ShapeDtypeStruct((4, 2, step, cols), BF16)
    out_spec = pl.BlockSpec((4, 1, step, cols), lambda e: (0, e, 0, 0))
    return pl.pallas_call(
        body,
        grid=(2,),
        in_specs=[pl.BlockSpec(memory_space=pltpu.SMEM)]
        + [pl.BlockSpec((1, slots, a.shape[2]), lambda e: (e, 0, 0)) for a in args],
        out_specs=[out_spec, out_spec],
        out_shape=[out, out],
        scratch_shapes=[pltpu.VMEM((rows, cols), F32)],
        compiler_params=pltpu.CompilerParams(vmem_limit_bytes=VMEM),
        cost_estimate=pl.CostEstimate(flops=4 * slots * rows * cols, bytes_accessed=16 << 20, transcendentals=0),
        name=name,
    )(where, *args)


def along_x(by):
    return [(x * 2 + c, (x + by) % 4 * 2 + c) for x in range(4) for c in range(2)]


def swap_cores(other):
    return lax.ppermute(other, "dp", [(x * 2 + c, x * 2 + 1 - c) for x in range(4) for c in range(2)])


def both(own, got, *at):
    return own[at].astype(F32) + got[at].astype(F32)


def send_far(own, got):
    return (
        lax.ppermute(both(own, got, 2, 0).astype(BF16), "dp", along_x(1)),
        lax.ppermute(both(own, got, 2, 1).astype(BF16), "dp", along_x(-1)),
    )


def send_near(own, got, far):
    ahead = jnp.stack([both(own, got, 1, 0) + far[0].astype(F32), both(own, got, 1, 1)]).astype(BF16)
    back = jnp.stack([both(own, got, 3, 0), both(own, got, 3, 1) + far[1].astype(F32)]).astype(BF16)
    ahead, back = lax.ppermute(ahead, "dp", along_x(1)), lax.ppermute(back, "dp", along_x(-1))
    return both(own, got, 0) + ahead.astype(F32) + back.astype(F32)


def along_y(by):
    return [(z * 4 + y, z * 4 + (y + by) % 4) for z in range(4) for y in range(4)]


def along_z(by):
    return [(z * 4 + y, (z + by) % 4 * 4 + y) for z in range(4) for y in range(4)]


def send(value, route):
    return lax.ppermute(value, "expert", route)


def gather_line(block, ring):
    half = block.shape[0] // 2
    back, ahead = send(block, ring(1)), send(block, ring(-1))
    far = [send(back[:half], ring(1)), send(ahead[half:], ring(-1))]
    return jnp.concatenate([block, *far], axis=0), jnp.concatenate([back, ahead], axis=0)


def tables(ids, first, my_z, my_y):
    mine = first + jnp.arange(2, dtype=jnp.int32)
    ids = ids.reshape(4, 4, SRC, TOP)
    ids = jnp.roll(ids, (-my_z, -my_y), (0, 1))
    ids = jnp.stack([ids[0], ids[2], ids[3], ids[1]])
    ids = jnp.stack([ids[:, 0], ids[:, 2], ids[:, 3], ids[:, 1]], axis=1)
    hit = jnp.any(ids[None] == mine[:, None, None, None, None], axis=4)
    before = jnp.triu(jnp.ones((SRC, SRC), BF16), 1)
    rank = jnp.einsum("ezyr,rs->ezys", hit.astype(BF16), before, preferred_element_type=F32).astype(jnp.int32)
    slot = jnp.where(hit, rank, -2 * PEER)

    def by_pairs(t):
        t = t.reshape(2, 4, 2, 2, SRC) + jnp.arange(2, dtype=jnp.int32)[:, None] * PEER
        return jnp.transpose(t, (1, 0, 2, 3, 4)).reshape(4, CHUNK, 2 * SRC)

    rel = jnp.pad((ids - first).reshape(4, 4 * SRC, TOP), ((0, 0), (0, 0), (0, LANES - TOP)), constant_values=-1)
    return by_pairs(slot), by_pairs(jnp.swapaxes(slot, 1, 2)), rel.astype(BF16)


def on_device(activations, out_grad, gate_probs, expert_ids, w_gate, w_up, w_down):
    my_index = lax.axis_index("expert")
    dp_index = lax.axis_index("dp")
    width = activations.shape[1]
    ff = w_gate.shape[2]
    my_z, my_y = my_index // 4, my_index % 4
    rows = jnp.concatenate([activations, jnp.pad(gate_probs, ((0, 0), (0, LANES - TOP)))], axis=1)
    tgt_x, tgt_g, rel = tables(expert_ids, my_index * 2, my_z, my_y)
    weights = (w_gate, w_up, w_down)
    x_own, g_own = lax.optimization_barrier((gather_line(rows, along_y), gather_line(out_grad, along_z)))
    (x_lo, x_hi), (g_lo, g_hi) = x_own, g_own
    onward = (
        send(x_hi, along_z(1)),
        send(x_lo, along_z(-1)),
        send(g_hi, along_y(1)),
        send(g_lo, along_y(-1)),
    )
    turned = turn_pass(w_gate, w_up)
    made = stage_pass(1, 0, (tgt_x, tgt_g, rel), x_own, g_own, weights, None)
    x_lo, x_hi, g_lo, g_hi, onward, turned, made = lax.optimization_barrier(
        (x_lo, x_hi, g_lo, g_hi, onward, turned, made)
    )
    x_near = send(x_lo, along_z(1)), onward[0], onward[1], send(x_hi, along_z(-1))
    g_near = send(g_lo, along_y(1)), onward[2], onward[3], send(g_hi, along_y(-1))
    x_far = send(onward[1], along_z(-1)), send(onward[0], along_z(1))
    g_far = send(onward[3], along_y(-1)), send(onward[2], along_y(1))
    made = stage_pass(2, 1, (tgt_x, tgt_g, rel), x_near, g_near, weights, made)
    away = jnp.array([0, 2, 3, 1], jnp.int32)
    place = jnp.concatenate([(my_z + away) % 4, (my_y + away) % 4]).astype(jnp.int32)
    xs, pa, gs, dhu, act = tail_pass(place, (tgt_x, tgt_g, rel), x_far, g_far, weights, turned, made)
    act_sum = lax.psum_scatter(act.reshape(16 * SRC, -1), "expert", scatter_dimension=0, tiled=True)
    where = jnp.stack([dp_index // 2, dp_index % 2]).astype(jnp.int32)
    flat = lambda v: v.reshape(2, 16 * PEER, -1)
    up = weight_pass(up_kernel, where, (flat(xs), dhu), width, 2 * ff, "up_grad")
    down = weight_pass(down_kernel, where, (flat(pa), flat(gs)), ff, width, "down_grad")
    got_up, got_down = swap_cores(up[0]), swap_cores(down[0])
    far_up = send_far(up[1], got_up)
    got_down, far_up = lax.optimization_barrier((got_down, far_up))
    far_down = send_far(down[1], got_down)
    grad_both = send_near(up[1], got_up, far_up)
    grad_down = send_near(down[1], got_down, far_down)
    return (
        act_sum[:, :width],
        act_sum[:, width : width + TOP].astype(F32),
        grad_both[:, :, :ff].astype(BF16),
        grad_both[:, :, ff:].astype(BF16),
        grad_down.astype(BF16),
    )


def solution(mesh):
    placed = (
        P(("dp", "expert"), None),
        P(("dp", "expert"), None),
        P(("dp", "expert"), None),
        P("dp", None),
        P("expert", None, None),
        P("expert", None, None),
        P("expert", None, None),
    )
    return jax.shard_map(
        on_device,
        mesh=mesh,
        in_specs=placed,
        out_specs=(
            P(("dp", "expert"), None),
            P(("dp", "expert"), None),
            P("expert", "dp", None),
            P("expert", "dp", None),
            P("expert", "dp", None),
        ),
        check_vma=False,
    )
```

```python
import functools

import jax
import jax.numpy as jnp
from jax import lax
from jax.experimental import pallas as pl
from jax.experimental.pallas import tpu as pltpu
from jax.sharding import PartitionSpec as P

TOP = 8
SRC = 128
CHUNK = 4
PEER = 48
LANES = 128
F32 = jnp.float32
BF16 = jnp.bfloat16

NT = (((1,), (1,)), ((), ()))
TN = (((0,), (0,)), ((), ()))


def dot(a, b, dims=(((1,), (0,)), ((), ()))):
    return lax.dot_general(a, b, dims, preferred_element_type=F32)
VMEM = 58 << 20


def hot(tgt, plane, pair):
    half = 2 * PEER
    places = lax.broadcasted_iota(jnp.int32, (half, 2 * SRC), 0)
    return jnp.concatenate(
        [(places == tgt[plane, e * 2 + pair, :][None, :]).astype(F32).astype(BF16) for e in range(2)], axis=0
    )


def pick_rows(n, tgt_x, tgt_g, rel, x, g, xs, gs, probs_of, picked):
    half = 2 * PEER
    slots = CHUNK * PEER
    width = xs.shape[3]
    for plane in range(n):
        for pair in range(2):
            spots = pl.ds(pair * half, half)
            pick = hot(tgt_x, plane, pair)
            rows = x[plane * 2 + pair]
            got = dot(pick, rows[:, pl.ds(0, width)]).astype(BF16)
            local = rel[plane, pl.ds(pair * 2 * SRC, 2 * SRC), :].astype(F32)
            probs = rows[:, pl.ds(width, LANES)].astype(F32)
            got_g = dot(hot(tgt_g, plane, pair), g[plane * 2 + pair][...]).astype(BF16)
            for e in range(2):
                part = slice(e * half, (e + 1) * half)
                xs[e, plane, spots, :] = got[part]
                picked[e, pl.ds(plane * slots + pair * half, half), :] = got_g[part]
                for i in range(2):
                    at = e * half + i * PEER
                    gs[e, pair * 2 + i, plane] = got_g[at : at + PEER]
                mine = jnp.where(local == e, probs, 0.0).astype(BF16)
                col = jnp.sum(dot(pick[part], mine), axis=1, keepdims=True)
                probs_of[e, pl.ds(plane * slots + pair * half, half), :] = jnp.broadcast_to(col, (half, LANES))


def products(rows, picked, p, wg, wu, wd):
    h = dot(rows, wg)
    u = dot(rows, wu)
    s = 1.0 / (1.0 + jnp.exp(-h))
    hs = h * s
    a = hs * u
    wp = p * (u * s * (1.0 + h * (1.0 - s)))
    return tuple(v.astype(BF16) for v in (p * a, a, wp, p * hs, dot(picked, wd, NT)))


def stage_kernel(n, tgt_x, tgt_g, rel, *refs):
    x, g, (wg, wu, wd) = refs[: 2 * n], refs[2 * n : 4 * n], refs[4 * n : 4 * n + 3]
    xs, pa, ab, wp, hp, gs, dap, probs_of, picked = refs[-9:]
    slots = CHUNK * PEER
    width, ff = wg.shape[1], wg.shape[2]
    e = pl.program_id(0)

    @pl.when(e == 0)
    def _():
        pick_rows(n, tgt_x, tgt_g, rel, x, g, xs, gs, probs_of, picked)

    rows = xs[e].reshape(n * slots, width)
    *made, back = products(rows, picked[e], probs_of[e][:, :1], wg[0], wu[0], wd[0])
    for out, value in zip((pa, ab, wp, hp), made):
        out[0] = value.reshape(n, slots, ff)
    for plane in range(n):
        for i in range(CHUNK):
            at = plane * slots + i * PEER
            dap[0, i, plane] = back[at : at + PEER]


def fixed(shape, *at):
    return pl.BlockSpec(shape, lambda e: at, pipeline_mode=pl.Buffered(1))


def by_expert(shape, *at):
    return pl.BlockSpec((1, *shape), lambda e: (e, *at))


def stage_pass(n, at, tables, x, g, weights, prior):
    wg, wu, wd = weights
    width, ff = wg.shape[1], wg.shape[2]
    slots = CHUNK * PEER
    by_plane = [width, ff, ff, ff, ff]
    by_line = [width, ff]
    held = [] if prior is None else list(prior)
    before = 3 + len(x) + len(g) + 3
    return pl.pallas_call(
        functools.partial(stage_kernel, n),
        grid=(2,),
        in_specs=[fixed((n, CHUNK, 2 * SRC), at, 0, 0)] * 2
        + [fixed((n, CHUNK * SRC, LANES), at, 0, 0)]
        + [fixed(v.shape, 0, 0) for v in (*x, *g)]
        + [by_expert(w.shape[1:], 0, 0) for w in weights]
        + [pl.BlockSpec(memory_space=pl.ANY)] * len(held),
        out_specs=[fixed((2, n, slots, width), 0, at, 0, 0)]
        + [by_expert((n, slots, ff), at, 0, 0)] * 4
        + [fixed((2, 4, n, PEER, width), 0, 0, at, 0, 0), by_expert((4, n, PEER, ff), 0, at, 0, 0)],
        out_shape=[jax.ShapeDtypeStruct((2, 4, slots, w), BF16) for w in by_plane]
        + [jax.ShapeDtypeStruct((2, 4, 4, PEER, w), BF16) for w in by_line],
        scratch_shapes=[pltpu.VMEM((2, n * slots, LANES), F32), pltpu.VMEM((2, n * slots, width), BF16)],
        input_output_aliases={before + i: i for i in range(len(held))},
        compiler_params=pltpu.CompilerParams(vmem_limit_bytes=VMEM),
        cost_estimate=pl.CostEstimate(flops=1 << 28, bytes_accessed=1 << 19, transcendentals=0),
        name="stage",
    )(*tables, *x, *g, *weights, *held)


def turn_kernel(wg, wu, out):
    ff = wg.shape[2]
    out[0, pl.ds(0, ff), :] = wg[0].T
    out[0, pl.ds(ff, ff), :] = wu[0].T


def turn_pass(wg, wu):
    width, ff = wg.shape[1], wg.shape[2]
    return pl.pallas_call(
        turn_kernel,
        grid=(2,),
        in_specs=[by_expert((width, ff), 0, 0)] * 2,
        out_specs=by_expert((2 * ff, width), 0, 0),
        out_shape=jax.ShapeDtypeStruct((2, 2 * ff, width), BF16),
        compiler_params=pltpu.CompilerParams(vmem_limit_bytes=VMEM),
        cost_estimate=pl.CostEstimate(flops=1 << 28, bytes_accessed=1 << 19, transcendentals=0),
        name="turn",
    )(wg, wu)


def weight_copies(e, given, kept, sem):
    return [pltpu.make_async_copy(g.at[e], k.at[e], sem.at[e, i]) for i, (g, k) in enumerate(zip(given, kept))]


def held_copies(held, kept, wt_hbm, wt, sem):
    copies = [(wt_hbm.at[e], wt.at[e]) for e in range(2)]
    for i, (src, dst) in enumerate(zip(held, kept)):
        for part in (pl.ds(0, 1), pl.ds(2, 2)):
            at = (slice(None), slice(None), part) if i == 3 else (slice(None), part)
            copies.append((src.at[at], dst.at[at]))
    return [pltpu.make_async_copy(src, dst, sem.at[i]) for i, (src, dst) in enumerate(copies)]


def tail_kernel(place, tgt_x, tgt_g, rel_x, tgt, rel, x_lo, x_hi, g_lo, g_hi, *refs):
    given, wt_hbm, held = refs[:3], refs[3], refs[7:11]
    xs, pa, gs, dhu, act, wg, wu, wd, wt, ab, wp, hp, dap, probs_of, picked, dxs, qs, weight_sem, sem = refs[11:]
    own, kept = (wg, wu, wd), (ab, wp, hp, dap)
    half = 2 * PEER
    slots = CHUNK * PEER
    width, ff = wg.shape[1], wg.shape[2]
    step = pl.program_id(0)

    @pl.when(step == 0)
    def _():
        for e in range(2):
            for copy in weight_copies(e, given, own, weight_sem):
                copy.start()
        for copy in held_copies(held, kept, wt_hbm, wt, sem):
            copy.start()
        pick_rows(1, tgt_x, tgt_g, rel_x, (x_lo, x_hi), (g_lo, g_hi), xs, gs, probs_of, picked)

    for e in range(2):

        @pl.when(step == e)
        def _():
            for copy in weight_copies(e, given, own, weight_sem):
                copy.wait()

    @pl.when(step < 2)
    def _():
        made = products(xs[step, 0], picked[step], probs_of[step][:, :1], wg[step], wu[step], wd[step])
        pa[0, 0] = made[0]
        for out, value in zip((ab, wp, hp), made[1:4]):
            out[step, 1] = value
        for i in range(CHUNK):
            dap[step, i, 1] = made[4][i * PEER : (i + 1) * PEER]

    @pl.when(step == 2)
    def _():
        for copy in held_copies(held, kept, wt_hbm, wt, sem):
            copy.wait()

    @pl.when(step >= 2)
    def _():
        k = step - 2
        for e in range(2):
            back = dap[e, k].astype(F32).reshape(slots, ff)
            q = jnp.sum(ab[e, k].astype(F32) * back, axis=1, keepdims=True)
            dhu[e, :, pl.ds(0, ff)] = (back * wp[e, k].astype(F32)).astype(BF16)
            dhu[e, :, pl.ds(ff, ff)] = (back * hp[e, k].astype(F32)).astype(BF16)
            wide = jnp.broadcast_to(q, (slots, LANES)).astype(BF16)
            for pair in range(2):
                qs[pair, pl.ds(e * half, half), :] = wide[pair * half : (pair + 1) * half]
        for e in range(2):
            dx = dot(dhu[e], wt[e]).astype(BF16)
            for pair in range(2):
                dxs[pair, pl.ds(e * half, half), :] = dx[pair * half : (pair + 1) * half]
        for pair in range(2):
            pick = hot(tgt, 0, pair)
            rows = dot(pick, dxs[pair], TN).astype(BF16)
            local = rel[0, pl.ds(pair * 2 * SRC, 2 * SRC), :].astype(F32)
            ext = jnp.zeros(local.shape, F32)
            for e in range(2):
                part = slice(e * half, (e + 1) * half)
                ext = ext + jnp.where(local == e, dot(pick[part], qs[pair, pl.ds(e * half, half), :], TN), 0.0)
            ext = ext.astype(BF16)
            for i in range(2):
                part = slice(i * SRC, (i + 1) * SRC)
                y = place[4 + pair * 2 + i]
                act[0, y, :, pl.ds(0, width)] = rows[part]
                act[0, y, :, pl.ds(width, LANES)] = ext[part]


def tail_pass(place, tables, x, g, weights, wt, made):
    tgt_x, tgt_g, rel = tables
    wg, wu, wd = weights
    width, ff = wg.shape[1], wg.shape[2]
    slots = CHUNK * PEER
    xs, pa, ab, wp, hp, gs, dap = made
    once = pl.Buffered(1)
    kept = lambda shape, *at: pl.BlockSpec(shape, lambda i, p: at, pipeline_mode=once)
    plane = lambda i: jnp.maximum(i - 2, 0)
    expert = lambda i: jnp.minimum(i, 1)
    of_plane = lambda *shape: pl.BlockSpec((1, *shape), lambda i, p: (plane(i), 0, 0))
    anywhere = pl.BlockSpec(memory_space=pl.ANY)
    return pl.pallas_call(
        tail_kernel,
        grid_spec=pltpu.PrefetchScalarGridSpec(
            num_scalar_prefetch=1,
            grid=(6,),
            in_specs=[
                kept((1, CHUNK, 2 * SRC), 1, 0, 0),
                kept((1, CHUNK, 2 * SRC), 1, 0, 0),
                kept((1, CHUNK * SRC, LANES), 1, 0, 0),
                of_plane(CHUNK, 2 * SRC),
                of_plane(CHUNK * SRC, LANES),
            ]
            + [kept(v.shape, 0, 0) for v in (*x, *g)]
            + [anywhere] * 11,
            out_specs=[
                kept((2, 1, slots, width), 0, 1, 0, 0),
                pl.BlockSpec((1, 1, slots, ff), lambda i, p: (expert(i), 1, 0, 0)),
                kept((2, 4, 1, PEER, width), 0, 0, 1, 0, 0),
                pl.BlockSpec((2, slots, 2 * ff), lambda i, p: (0, plane(i), 0)),
                pl.BlockSpec((1, 4, SRC, width + LANES), lambda i, p: (p[plane(i)], 0, 0, 0)),
            ],
            scratch_shapes=[pltpu.VMEM(w.shape, BF16) for w in weights]
            + [
                pltpu.VMEM(wt.shape, BF16),
                pltpu.VMEM(ab.shape, BF16),
                pltpu.VMEM(wp.shape, BF16),
                pltpu.VMEM(hp.shape, BF16),
                pltpu.VMEM(dap.shape, BF16),
                pltpu.VMEM((2, slots, LANES), F32),
                pltpu.VMEM((2, slots, width), BF16),
                pltpu.VMEM((2, 4 * PEER, width), BF16),
                pltpu.VMEM((2, 4 * PEER, LANES), BF16),
                pltpu.SemaphoreType.DMA((2, 3)),
                pltpu.SemaphoreType.DMA((10,)),
            ],
        ),
        out_shape=[jax.ShapeDtypeStruct(v.shape, BF16) for v in (xs, pa, gs)]
        + [
            jax.ShapeDtypeStruct((2, 4 * slots, 2 * ff), BF16),
            jax.ShapeDtypeStruct((4, 4, SRC, width + LANES), BF16),
        ],
        input_output_aliases={14: 0, 15: 1, 16: 2},
        compiler_params=pltpu.CompilerParams(vmem_limit_bytes=VMEM),
        cost_estimate=pl.CostEstimate(flops=14 << 30, bytes_accessed=32 << 20, transcendentals=0),
        name="tail",
    )(place, tgt_x, tgt_g, rel, tgt_x, rel, *x, *g, wg, wu, wd, wt, xs, pa, gs, ab, wp, hp, dap)


def place_chunks(where, total, outs, step):
    my_x, my_c = where[0], where[1]
    for ahead in range(4):
        for own in range(2):
            core = my_c if own else 1 - my_c
            piece = lax.rem(my_x + ahead, 4) * 2 + core
            start = pl.multiple_of(piece * step, step)
            outs[own][ahead, 0] = total[pl.ds(start, step), :].astype(BF16)


def down_kernel(where, pa, gs, other, own, total):
    total[...] = dot(pa[0], gs[0], TN)
    place_chunks(where, total, (other, own), total.shape[0] // 8)


def up_kernel(where, xs, dhu, other, own, total):
    total[...] = dot(xs[0], dhu[0], TN)
    place_chunks(where, total, (other, own), total.shape[0] // 8)


def weight_pass(body, where, args, rows, cols, name):
    slots = args[0].shape[1]
    step = rows // 8
    out = jax.ShapeDtypeStruct((4, 2, step, cols), BF16)
    out_spec = pl.BlockSpec((4, 1, step, cols), lambda e: (0, e, 0, 0))
    return pl.pallas_call(
        body,
        grid=(2,),
        in_specs=[pl.BlockSpec(memory_space=pltpu.SMEM)]
        + [pl.BlockSpec((1, slots, a.shape[2]), lambda e: (e, 0, 0)) for a in args],
        out_specs=[out_spec, out_spec],
        out_shape=[out, out],
        scratch_shapes=[pltpu.VMEM((rows, cols), F32)],
        compiler_params=pltpu.CompilerParams(vmem_limit_bytes=VMEM),
        cost_estimate=pl.CostEstimate(flops=4 * slots * rows * cols, bytes_accessed=16 << 20, transcendentals=0),
        name=name,
    )(where, *args)


def along_x(by):
    return [(x * 2 + c, (x + by) % 4 * 2 + c) for x in range(4) for c in range(2)]


def swap_cores(other):
    return lax.ppermute(other, "dp", [(x * 2 + c, x * 2 + 1 - c) for x in range(4) for c in range(2)])


def both(own, got, *at):
    return own[at].astype(F32) + got[at].astype(F32)


def send_far(own, got):
    return (
        lax.ppermute(both(own, got, 2, 0).astype(BF16), "dp", along_x(1)),
        lax.ppermute(both(own, got, 2, 1).astype(BF16), "dp", along_x(-1)),
    )


def send_near(own, got, far):
    ahead = jnp.stack([both(own, got, 1, 0) + far[0].astype(F32), both(own, got, 1, 1)]).astype(BF16)
    back = jnp.stack([both(own, got, 3, 0), both(own, got, 3, 1) + far[1].astype(F32)]).astype(BF16)
    ahead, back = lax.ppermute(ahead, "dp", along_x(1)), lax.ppermute(back, "dp", along_x(-1))
    return both(own, got, 0) + ahead.astype(F32) + back.astype(F32)


def split_kernel(both, rows, probs):
    width = rows.shape[1]
    rows[...] = both[:, pl.ds(0, width)]
    probs[...] = both[:, pl.ds(width, LANES)].astype(F32)[:, : probs.shape[1]]


def split_pass(both, width):
    count = both.shape[0]
    return pl.pallas_call(
        split_kernel,
        out_shape=[jax.ShapeDtypeStruct((count, width), BF16), jax.ShapeDtypeStruct((count, TOP), F32)],
        cost_estimate=pl.CostEstimate(flops=0, bytes_accessed=1 << 20, transcendentals=0),
        name="split",
    )(both)


def along_y(by):
    return [(z * 4 + y, z * 4 + (y + by) % 4) for z in range(4) for y in range(4)]


def along_z(by):
    return [(z * 4 + y, (z + by) % 4 * 4 + y) for z in range(4) for y in range(4)]


def send(value, route):
    return lax.ppermute(value, "expert", route)


def gather_line(block, ring):
    back, ahead, far = send(block, ring(1)), send(block, ring(-1)), send(block, ring(2))
    return jnp.concatenate([block, far], axis=0), jnp.concatenate([back, ahead], axis=0)


def tables(ids, first, my_z, my_y):
    mine = first + jnp.arange(2, dtype=jnp.int32)
    ids = ids.reshape(4, 4, SRC, TOP)
    ids = jnp.roll(ids, (-my_z, -my_y), (0, 1))
    ids = jnp.stack([ids[0], ids[2], ids[3], ids[1]])
    ids = jnp.stack([ids[:, 0], ids[:, 2], ids[:, 3], ids[:, 1]], axis=1)
    hit = jnp.any(ids[None] == mine[:, None, None, None, None], axis=4)
    before = jnp.triu(jnp.ones((SRC, SRC), BF16), 1)
    rank = jnp.einsum("ezyr,rs->ezys", hit.astype(BF16), before, preferred_element_type=F32).astype(jnp.int32)
    slot = jnp.where(hit, rank, -2 * PEER)

    def by_pairs(t):
        t = t.reshape(2, 4, 2, 2, SRC) + jnp.arange(2, dtype=jnp.int32)[:, None] * PEER
        return jnp.transpose(t, (1, 0, 2, 3, 4)).reshape(4, CHUNK, 2 * SRC)

    rel = jnp.pad((ids - first).reshape(4, 4 * SRC, TOP), ((0, 0), (0, 0), (0, LANES - TOP)), constant_values=-1)
    return by_pairs(slot), by_pairs(jnp.swapaxes(slot, 1, 2)), rel.astype(BF16)


def on_device(activations, out_grad, gate_probs, expert_ids, w_gate, w_up, w_down):
    my_index = lax.axis_index("expert")
    dp_index = lax.axis_index("dp")
    width = activations.shape[1]
    ff = w_gate.shape[2]
    my_z, my_y = my_index // 4, my_index % 4
    rows = jnp.concatenate([activations, jnp.pad(gate_probs, ((0, 0), (0, LANES - TOP)))], axis=1)
    tgt_x, tgt_g, rel = tables(expert_ids, my_index * 2, my_z, my_y)
    weights = (w_gate, w_up, w_down)
    x_own, g_own = lax.optimization_barrier((gather_line(rows, along_y), gather_line(out_grad, along_z)))
    (x_lo, x_hi), (g_lo, g_hi) = x_own, g_own
    onward = (
        send(x_hi, along_z(1)),
        send(x_lo, along_z(-1)),
        send(g_hi, along_y(1)),
        send(g_lo, along_y(-1)),
    )
    turned = turn_pass(w_gate, w_up)
    made = stage_pass(1, 0, (tgt_x, tgt_g, rel), x_own, g_own, weights, None)
    x_lo, x_hi, g_lo, g_hi, onward, turned, made = lax.optimization_barrier(
        (x_lo, x_hi, g_lo, g_hi, onward, turned, made)
    )
    x_near = send(x_lo, along_z(1)), onward[0], onward[1], send(x_hi, along_z(-1))
    g_near = send(g_lo, along_y(1)), onward[2], onward[3], send(g_hi, along_y(-1))
    x_far = send(onward[1], along_z(-1)), send(onward[0], along_z(1))
    g_far = send(onward[3], along_y(-1)), send(onward[2], along_y(1))
    made = stage_pass(2, 1, (tgt_x, tgt_g, rel), x_near, g_near, weights, made)
    away = jnp.array([0, 2, 3, 1], jnp.int32)
    place = jnp.concatenate([(my_z + away) % 4, (my_y + away) % 4]).astype(jnp.int32)
    xs, pa, gs, dhu, act = tail_pass(place, (tgt_x, tgt_g, rel), x_far, g_far, weights, turned, made)
    act_sum = lax.psum_scatter(act.reshape(16 * SRC, -1), "expert", scatter_dimension=0, tiled=True)
    where = jnp.stack([dp_index // 2, dp_index % 2]).astype(jnp.int32)
    flat = lambda v: v.reshape(2, 16 * PEER, -1)
    up = weight_pass(up_kernel, where, (flat(xs), dhu), width, 2 * ff, "up_grad")
    down = weight_pass(down_kernel, where, (flat(pa), flat(gs)), ff, width, "down_grad")
    got_up, got_down = swap_cores(up[0]), swap_cores(down[0])
    far_up = send_far(up[1], got_up)
    got_down, far_up = lax.optimization_barrier((got_down, far_up))
    far_down = send_far(down[1], got_down)
    grad_both = send_near(up[1], got_up, far_up)
    grad_down = send_near(down[1], got_down, far_down)
    grad_act, grad_prob = split_pass(act_sum, width)
    return (
        grad_act,
        grad_prob,
        grad_both[:, :, :ff].astype(BF16),
        grad_both[:, :, ff:].astype(BF16),
        grad_down.astype(BF16),
    )


def solution(mesh):
    placed = (
        P(("dp", "expert"), None),
        P(("dp", "expert"), None),
        P(("dp", "expert"), None),
        P("dp", None),
        P("expert", None, None),
        P("expert", None, None),
        P("expert", None, None),
    )
    return jax.shard_map(
        on_device,
        mesh=mesh,
        in_specs=placed,
        out_specs=(
            P(("dp", "expert"), None),
            P(("dp", "expert"), None),
            P("expert", "dp", None),
            P("expert", "dp", None),
            P("expert", "dp", None),
        ),
        check_vma=False,
    )
```

```python
import functools

import jax
import jax.numpy as jnp
from jax import lax
from jax.experimental import pallas as pl
from jax.experimental.pallas import tpu as pltpu
from jax.sharding import PartitionSpec as P

TOP = 8
SRC = 128
CHUNK = 4
PEER = 48
LANES = 128
F32 = jnp.float32
BF16 = jnp.bfloat16

NT = (((1,), (1,)), ((), ()))
TN = (((0,), (0,)), ((), ()))


def dot(a, b, dims=(((1,), (0,)), ((), ()))):
    return lax.dot_general(a, b, dims, preferred_element_type=F32)
VMEM = 58 << 20


def hot(tgt, plane, pair):
    half = 2 * PEER
    places = lax.broadcasted_iota(jnp.int32, (half, 2 * SRC), 0)
    return jnp.concatenate(
        [(places == tgt[plane, e * 2 + pair, :][None, :]).astype(F32).astype(BF16) for e in range(2)], axis=0
    )


def pick_rows(n, tgt_x, tgt_g, rel, x, g, xs, gs, probs_of, picked):
    half = 2 * PEER
    slots = CHUNK * PEER
    width = xs.shape[3]
    for plane in range(n):
        for pair in range(2):
            spots = pl.ds(pair * half, half)
            pick = hot(tgt_x, plane, pair)
            rows = x[plane * 2 + pair]
            got = dot(pick, rows[:, pl.ds(0, width)]).astype(BF16)
            local = rel[plane, pl.ds(pair * 2 * SRC, 2 * SRC), :].astype(F32)
            probs = rows[:, pl.ds(width, LANES)].astype(F32)
            got_g = dot(hot(tgt_g, plane, pair), g[plane * 2 + pair][...]).astype(BF16)
            for e in range(2):
                part = slice(e * half, (e + 1) * half)
                xs[e, plane, spots, :] = got[part]
                picked[e, pl.ds(plane * slots + pair * half, half), :] = got_g[part]
                for i in range(2):
                    at = e * half + i * PEER
                    gs[e, pair * 2 + i, plane] = got_g[at : at + PEER]
                mine = jnp.where(local == e, probs, 0.0).astype(BF16)
                col = jnp.sum(dot(pick[part], mine), axis=1, keepdims=True)
                probs_of[e, pl.ds(plane * slots + pair * half, half), :] = jnp.broadcast_to(col, (half, LANES))


def products(rows, picked, p, wg, wu, wd):
    h = dot(rows, wg)
    u = dot(rows, wu)
    s = 1.0 / (1.0 + jnp.exp(-h))
    hs = h * s
    a = hs * u
    wp = p * (u * s * (1.0 + h * (1.0 - s)))
    return tuple(v.astype(BF16) for v in (p * a, a, wp, p * hs, dot(picked, wd, NT)))


def stage_kernel(n, tgt_x, tgt_g, rel, *refs):
    x, g, (wg, wu, wd) = refs[: 2 * n], refs[2 * n : 4 * n], refs[4 * n : 4 * n + 3]
    xs, pa, ab, wp, hp, gs, dap, probs_of, picked = refs[-9:]
    slots = CHUNK * PEER
    width, ff = wg.shape[1], wg.shape[2]
    e = pl.program_id(0)

    @pl.when(e == 0)
    def _():
        pick_rows(n, tgt_x, tgt_g, rel, x, g, xs, gs, probs_of, picked)

    rows = xs[e].reshape(n * slots, width)
    *made, back = products(rows, picked[e], probs_of[e][:, :1], wg[0], wu[0], wd[0])
    for out, value in zip((pa, ab, wp, hp), made):
        out[0] = value.reshape(n, slots, ff)
    for plane in range(n):
        for i in range(CHUNK):
            at = plane * slots + i * PEER
            dap[0, i, plane] = back[at : at + PEER]


def fixed(shape, *at):
    return pl.BlockSpec(shape, lambda e: at, pipeline_mode=pl.Buffered(1))


def by_expert(shape, *at):
    return pl.BlockSpec((1, *shape), lambda e: (e, *at))


def stage_pass(n, at, tables, x, g, weights, prior):
    wg, wu, wd = weights
    width, ff = wg.shape[1], wg.shape[2]
    slots = CHUNK * PEER
    by_plane = [width, ff, ff, ff, ff]
    by_line = [width, ff]
    held = [] if prior is None else list(prior)
    before = 3 + len(x) + len(g) + 3
    return pl.pallas_call(
        functools.partial(stage_kernel, n),
        grid=(2,),
        in_specs=[fixed((n, CHUNK, 2 * SRC), at, 0, 0)] * 2
        + [fixed((n, CHUNK * SRC, LANES), at, 0, 0)]
        + [fixed(v.shape, 0, 0) for v in (*x, *g)]
        + [by_expert(w.shape[1:], 0, 0) for w in weights]
        + [pl.BlockSpec(memory_space=pl.ANY)] * len(held),
        out_specs=[fixed((2, n, slots, width), 0, at, 0, 0)]
        + [by_expert((n, slots, ff), at, 0, 0)] * 4
        + [fixed((2, 4, n, PEER, width), 0, 0, at, 0, 0), by_expert((4, n, PEER, ff), 0, at, 0, 0)],
        out_shape=[jax.ShapeDtypeStruct((2, 4, slots, w), BF16) for w in by_plane]
        + [jax.ShapeDtypeStruct((2, 4, 4, PEER, w), BF16) for w in by_line],
        scratch_shapes=[pltpu.VMEM((2, n * slots, LANES), F32), pltpu.VMEM((2, n * slots, width), BF16)],
        input_output_aliases={before + i: i for i in range(len(held))},
        compiler_params=pltpu.CompilerParams(vmem_limit_bytes=VMEM),
        cost_estimate=pl.CostEstimate(flops=1 << 28, bytes_accessed=1 << 19, transcendentals=0),
        name="stage",
    )(*tables, *x, *g, *weights, *held)


def turn_kernel(wg, wu, out):
    ff = wg.shape[2]
    out[0, pl.ds(0, ff), :] = wg[0].T
    out[0, pl.ds(ff, ff), :] = wu[0].T


def turn_pass(wg, wu):
    width, ff = wg.shape[1], wg.shape[2]
    return pl.pallas_call(
        turn_kernel,
        grid=(2,),
        in_specs=[by_expert((width, ff), 0, 0)] * 2,
        out_specs=by_expert((2 * ff, width), 0, 0),
        out_shape=jax.ShapeDtypeStruct((2, 2 * ff, width), BF16),
        compiler_params=pltpu.CompilerParams(vmem_limit_bytes=VMEM),
        cost_estimate=pl.CostEstimate(flops=1 << 28, bytes_accessed=1 << 19, transcendentals=0),
        name="turn",
    )(wg, wu)


def expert_copies(e, given, kept, sem):
    return [pltpu.make_async_copy(g.at[e], k.at[e], sem.at[e, i]) for i, (g, k) in enumerate(zip(given, kept))]


def held_copies(held, kept, sem):
    copies = []
    for i, (src, dst) in enumerate(zip(held, kept)):
        for part in (pl.ds(0, 1), pl.ds(2, 2)):
            at = (slice(None), slice(None), part) if i == 3 else (slice(None), part)
            copies.append((src.at[at], dst.at[at]))
    return [pltpu.make_async_copy(src, dst, sem.at[i]) for i, (src, dst) in enumerate(copies)]


def tail_kernel(place, tgt_x, tgt_g, rel_x, tgt, rel, x_lo, x_hi, g_lo, g_hi, *refs):
    given, wt_hbm, held = refs[:3], refs[3:4], refs[7:11]
    xs, pa, gs, dhu, act, wg, wu, wd, wt, ab, wp, hp, dap, probs_of, picked, dxs, qs, in_sem, out_sem, sem = refs[11:]
    own, kept = (wg, wu, wd), (ab, wp, hp, dap)
    half = 2 * PEER
    slots = CHUNK * PEER
    width, ff = wg.shape[1], wg.shape[2]
    step = pl.program_id(0)

    @pl.when(step == 0)
    def _():
        for copy in expert_copies(0, given, own, in_sem):
            copy.start()
        pick_rows(1, tgt_x, tgt_g, rel_x, (x_lo, x_hi), (g_lo, g_hi), xs, gs, probs_of, picked)
        for copy in expert_copies(0, given, own, in_sem):
            copy.wait()
        for copy in expert_copies(1, given, own, in_sem) + held_copies(held, kept, sem):
            copy.start()

    @pl.when(step == 1)
    def _():
        for copy in expert_copies(1, given, own, in_sem):
            copy.wait()
        for e in range(2):
            for copy in expert_copies(e, wt_hbm, (wt,), out_sem):
                copy.start()

    @pl.when(step < 2)
    def _():
        made = products(xs[step, 0], picked[step], probs_of[step][:, :1], wg[step], wu[step], wd[step])
        pa[0, 0] = made[0]
        for out, value in zip((ab, wp, hp), made[1:4]):
            out[step, 1] = value
        for i in range(CHUNK):
            dap[step, i, 1] = made[4][i * PEER : (i + 1) * PEER]

    @pl.when(step == 2)
    def _():
        for copy in held_copies(held, kept, sem):
            copy.wait()

    @pl.when(step >= 2)
    def _():
        k = step - 2
        for e in range(2):
            back = dap[e, k].astype(F32).reshape(slots, ff)
            q = jnp.sum(ab[e, k].astype(F32) * back, axis=1, keepdims=True)
            dhu[e, :, pl.ds(0, ff)] = (back * wp[e, k].astype(F32)).astype(BF16)
            dhu[e, :, pl.ds(ff, ff)] = (back * hp[e, k].astype(F32)).astype(BF16)
            wide = jnp.broadcast_to(q, (slots, LANES)).astype(BF16)
            for pair in range(2):
                qs[pair, pl.ds(e * half, half), :] = wide[pair * half : (pair + 1) * half]
        for e in range(2):

            @pl.when(k == 0)
            def _():
                for copy in expert_copies(e, wt_hbm, (wt,), out_sem):
                    copy.wait()

            dx = dot(dhu[e], wt[e]).astype(BF16)
            for pair in range(2):
                dxs[pair, pl.ds(e * half, half), :] = dx[pair * half : (pair + 1) * half]
        for pair in range(2):
            pick = hot(tgt, 0, pair)
            rows = dot(pick, dxs[pair], TN).astype(BF16)
            local = rel[0, pl.ds(pair * 2 * SRC, 2 * SRC), :].astype(F32)
            ext = jnp.zeros(local.shape, F32)
            for e in range(2):
                part = slice(e * half, (e + 1) * half)
                ext = ext + jnp.where(local == e, dot(pick[part], qs[pair, pl.ds(e * half, half), :], TN), 0.0)
            ext = ext.astype(BF16)
            for i in range(2):
                part = slice(i * SRC, (i + 1) * SRC)
                y = place[4 + pair * 2 + i]
                act[0, y, :, pl.ds(0, width)] = rows[part]
                act[0, y, :, pl.ds(width, LANES)] = ext[part]


def tail_pass(place, tables, x, g, weights, wt, made):
    tgt_x, tgt_g, rel = tables
    wg, wu, wd = weights
    width, ff = wg.shape[1], wg.shape[2]
    slots = CHUNK * PEER
    xs, pa, ab, wp, hp, gs, dap = made
    once = pl.Buffered(1)
    kept = lambda shape, *at: pl.BlockSpec(shape, lambda i, p: at, pipeline_mode=once)
    plane = lambda i: jnp.maximum(i - 2, 0)
    expert = lambda i: jnp.minimum(i, 1)
    of_plane = lambda *shape: pl.BlockSpec((1, *shape), lambda i, p: (plane(i), 0, 0))
    anywhere = pl.BlockSpec(memory_space=pl.ANY)
    return pl.pallas_call(
        tail_kernel,
        grid_spec=pltpu.PrefetchScalarGridSpec(
            num_scalar_prefetch=1,
            grid=(6,),
            in_specs=[
                kept((1, CHUNK, 2 * SRC), 1, 0, 0),
                kept((1, CHUNK, 2 * SRC), 1, 0, 0),
                kept((1, CHUNK * SRC, LANES), 1, 0, 0),
                of_plane(CHUNK, 2 * SRC),
                of_plane(CHUNK * SRC, LANES),
            ]
            + [kept(v.shape, 0, 0) for v in (*x, *g)]
            + [anywhere] * 11,
            out_specs=[
                kept((2, 1, slots, width), 0, 1, 0, 0),
                pl.BlockSpec((1, 1, slots, ff), lambda i, p: (expert(i), 1, 0, 0)),
                kept((2, 4, 1, PEER, width), 0, 0, 1, 0, 0),
                pl.BlockSpec((2, slots, 2 * ff), lambda i, p: (0, plane(i), 0)),
                pl.BlockSpec((1, 4, SRC, width + LANES), lambda i, p: (p[plane(i)], 0, 0, 0)),
            ],
            scratch_shapes=[pltpu.VMEM(w.shape, BF16) for w in weights]
            + [
                pltpu.VMEM(wt.shape, BF16),
                pltpu.VMEM(ab.shape, BF16),
                pltpu.VMEM(wp.shape, BF16),
                pltpu.VMEM(hp.shape, BF16),
                pltpu.VMEM(dap.shape, BF16),
                pltpu.VMEM((2, slots, LANES), F32),
                pltpu.VMEM((2, slots, width), BF16),
                pltpu.VMEM((2, 4 * PEER, width), BF16),
                pltpu.VMEM((2, 4 * PEER, LANES), BF16),
                pltpu.SemaphoreType.DMA((2, 3)),
                pltpu.SemaphoreType.DMA((2, 1)),
                pltpu.SemaphoreType.DMA((8,)),
            ],
        ),
        out_shape=[jax.ShapeDtypeStruct(v.shape, BF16) for v in (xs, pa, gs)]
        + [
            jax.ShapeDtypeStruct((2, 4 * slots, 2 * ff), BF16),
            jax.ShapeDtypeStruct((4, 4, SRC, width + LANES), BF16),
        ],
        input_output_aliases={14: 0, 15: 1, 16: 2},
        compiler_params=pltpu.CompilerParams(vmem_limit_bytes=VMEM),
        cost_estimate=pl.CostEstimate(flops=14 << 30, bytes_accessed=32 << 20, transcendentals=0),
        name="tail",
    )(place, tgt_x, tgt_g, rel, tgt_x, rel, *x, *g, wg, wu, wd, wt, xs, pa, gs, ab, wp, hp, dap)


def place_chunks(where, total, outs, step):
    my_x, my_c = where[0], where[1]
    for ahead in range(4):
        for own in range(2):
            core = my_c if own else 1 - my_c
            piece = lax.rem(my_x + ahead, 4) * 2 + core
            start = pl.multiple_of(piece * step, step)
            outs[own][ahead, 0] = total[pl.ds(start, step), :].astype(BF16)


def down_kernel(where, pa, gs, other, own, total):
    total[...] = dot(pa[0], gs[0], TN)
    place_chunks(where, total, (other, own), total.shape[0] // 8)


def up_kernel(where, xs, dhu, other, own, total):
    total[...] = dot(xs[0], dhu[0], TN)
    place_chunks(where, total, (other, own), total.shape[0] // 8)


def weight_pass(body, where, args, rows, cols, name):
    slots = args[0].shape[1]
    step = rows // 8
    out = jax.ShapeDtypeStruct((4, 2, step, cols), BF16)
    out_spec = pl.BlockSpec((4, 1, step, cols), lambda e: (0, e, 0, 0))
    return pl.pallas_call(
        body,
        grid=(2,),
        in_specs=[pl.BlockSpec(memory_space=pltpu.SMEM)]
        + [pl.BlockSpec((1, slots, a.shape[2]), lambda e: (e, 0, 0)) for a in args],
        out_specs=[out_spec, out_spec],
        out_shape=[out, out],
        scratch_shapes=[pltpu.VMEM((rows, cols), F32)],
        compiler_params=pltpu.CompilerParams(vmem_limit_bytes=VMEM),
        cost_estimate=pl.CostEstimate(flops=4 * slots * rows * cols, bytes_accessed=16 << 20, transcendentals=0),
        name=name,
    )(where, *args)


def along_x(by):
    return [(x * 2 + c, (x + by) % 4 * 2 + c) for x in range(4) for c in range(2)]


def swap_cores(other):
    return lax.ppermute(other, "dp", [(x * 2 + c, x * 2 + 1 - c) for x in range(4) for c in range(2)])


def both(own, got, *at):
    return own[at].astype(F32) + got[at].astype(F32)


def send_far(own, got):
    return (
        lax.ppermute(both(own, got, 2, 0).astype(BF16), "dp", along_x(1)),
        lax.ppermute(both(own, got, 2, 1).astype(BF16), "dp", along_x(-1)),
    )


def send_near(own, got, far):
    ahead = jnp.stack([both(own, got, 1, 0) + far[0].astype(F32), both(own, got, 1, 1)]).astype(BF16)
    back = jnp.stack([both(own, got, 3, 0), both(own, got, 3, 1) + far[1].astype(F32)]).astype(BF16)
    ahead, back = lax.ppermute(ahead, "dp", along_x(1)), lax.ppermute(back, "dp", along_x(-1))
    return both(own, got, 0) + ahead.astype(F32) + back.astype(F32)


def along_y(by):
    return [(z * 4 + y, z * 4 + (y + by) % 4) for z in range(4) for y in range(4)]


def along_z(by):
    return [(z * 4 + y, (z + by) % 4 * 4 + y) for z in range(4) for y in range(4)]


def send(value, route):
    return lax.ppermute(value, "expert", route)


def gather_line(block, ring):
    half = block.shape[0] // 2
    back, ahead = send(block, ring(1)), send(block, ring(-1))
    far = [send(back[:half], ring(1)), send(ahead[half:], ring(-1))]
    return jnp.concatenate([block, *far], axis=0), jnp.concatenate([back, ahead], axis=0)


def tables(ids, first, my_z, my_y):
    mine = first + jnp.arange(2, dtype=jnp.int32)
    ids = ids.reshape(4, 4, SRC, TOP)
    ids = jnp.roll(ids, (-my_z, -my_y), (0, 1))
    ids = jnp.stack([ids[0], ids[2], ids[3], ids[1]])
    ids = jnp.stack([ids[:, 0], ids[:, 2], ids[:, 3], ids[:, 1]], axis=1)
    hit = jnp.any(ids[None] == mine[:, None, None, None, None], axis=4)
    before = jnp.triu(jnp.ones((SRC, SRC), BF16), 1)
    rank = jnp.einsum("ezyr,rs->ezys", hit.astype(BF16), before, preferred_element_type=F32).astype(jnp.int32)
    slot = jnp.where(hit, rank, -2 * PEER)

    def by_pairs(t):
        t = t.reshape(2, 4, 2, 2, SRC) + jnp.arange(2, dtype=jnp.int32)[:, None] * PEER
        return jnp.transpose(t, (1, 0, 2, 3, 4)).reshape(4, CHUNK, 2 * SRC)

    rel = jnp.pad((ids - first).reshape(4, 4 * SRC, TOP), ((0, 0), (0, 0), (0, LANES - TOP)), constant_values=-1)
    return by_pairs(slot), by_pairs(jnp.swapaxes(slot, 1, 2)), rel.astype(BF16)


def on_device(activations, out_grad, gate_probs, expert_ids, w_gate, w_up, w_down):
    my_index = lax.axis_index("expert")
    dp_index = lax.axis_index("dp")
    width = activations.shape[1]
    ff = w_gate.shape[2]
    my_z, my_y = my_index // 4, my_index % 4
    rows = jnp.concatenate([activations, jnp.pad(gate_probs, ((0, 0), (0, LANES - TOP)))], axis=1)
    tgt_x, tgt_g, rel = tables(expert_ids, my_index * 2, my_z, my_y)
    weights = (w_gate, w_up, w_down)
    x_own, g_own = lax.optimization_barrier((gather_line(rows, along_y), gather_line(out_grad, along_z)))
    (x_lo, x_hi), (g_lo, g_hi) = x_own, g_own
    onward = (
        send(x_hi, along_z(1)),
        send(x_lo, along_z(-1)),
        send(g_hi, along_y(1)),
        send(g_lo, along_y(-1)),
    )
    turned = turn_pass(w_gate, w_up)
    made = stage_pass(1, 0, (tgt_x, tgt_g, rel), x_own, g_own, weights, None)
    x_lo, x_hi, g_lo, g_hi, onward, turned, made = lax.optimization_barrier(
        (x_lo, x_hi, g_lo, g_hi, onward, turned, made)
    )
    x_near = send(x_lo, along_z(1)), onward[0], onward[1], send(x_hi, along_z(-1))
    g_near = send(g_lo, along_y(1)), onward[2], onward[3], send(g_hi, along_y(-1))
    x_far = send(onward[1], along_z(-1)), send(onward[0], along_z(1))
    g_far = send(onward[3], along_y(-1)), send(onward[2], along_y(1))
    made = stage_pass(2, 1, (tgt_x, tgt_g, rel), x_near, g_near, weights, made)
    away = jnp.array([0, 2, 3, 1], jnp.int32)
    place = jnp.concatenate([(my_z + away) % 4, (my_y + away) % 4]).astype(jnp.int32)
    xs, pa, gs, dhu, act = tail_pass(place, (tgt_x, tgt_g, rel), x_far, g_far, weights, turned, made)
    act_sum = lax.psum_scatter(act.reshape(16 * SRC, -1), "expert", scatter_dimension=0, tiled=True)
    where = jnp.stack([dp_index // 2, dp_index % 2]).astype(jnp.int32)
    flat = lambda v: v.reshape(2, 16 * PEER, -1)
    up = weight_pass(up_kernel, where, (flat(xs), dhu), width, 2 * ff, "up_grad")
    down = weight_pass(down_kernel, where, (flat(pa), flat(gs)), ff, width, "down_grad")
    got_up, got_down = swap_cores(up[0]), swap_cores(down[0])
    far_up = send_far(up[1], got_up)
    got_down, far_up = lax.optimization_barrier((got_down, far_up))
    far_down = send_far(down[1], got_down)
    grad_both = send_near(up[1], got_up, far_up)
    grad_down = send_near(down[1], got_down, far_down)
    return (
        act_sum[:, :width],
        act_sum[:, width : width + TOP].astype(F32),
        grad_both[:, :, :ff].astype(BF16),
        grad_both[:, :, ff:].astype(BF16),
        grad_down.astype(BF16),
    )


def solution(mesh):
    placed = (
        P(("dp", "expert"), None),
        P(("dp", "expert"), None),
        P(("dp", "expert"), None),
        P("dp", None),
        P("expert", None, None),
        P("expert", None, None),
        P("expert", None, None),
    )
    return jax.shard_map(
        on_device,
        mesh=mesh,
        in_specs=placed,
        out_specs=(
            P(("dp", "expert"), None),
            P(("dp", "expert"), None),
            P("expert", "dp", None),
            P("expert", "dp", None),
            P("expert", "dp", None),
        ),
        check_vma=False,
    )
```

```python
import functools

import jax
import jax.numpy as jnp
from jax import lax
from jax.experimental import pallas as pl
from jax.experimental.pallas import tpu as pltpu
from jax.sharding import PartitionSpec as P

TOP = 8
SRC = 128
CHUNK = 4
PEER = 48
LANES = 128
F32 = jnp.float32
BF16 = jnp.bfloat16

NT = (((1,), (1,)), ((), ()))
TN = (((0,), (0,)), ((), ()))


def dot(a, b, dims=(((1,), (0,)), ((), ()))):
    return lax.dot_general(a, b, dims, preferred_element_type=F32)
VMEM = 58 << 20


def hot(tgt, plane, pair):
    half = 2 * PEER
    places = lax.broadcasted_iota(jnp.int32, (half, 2 * SRC), 0)
    return jnp.concatenate(
        [(places == tgt[plane, e * 2 + pair, :][None, :]).astype(F32).astype(BF16) for e in range(2)], axis=0
    )


def pick_rows(n, tgt_x, tgt_g, rel, x, g, xs, gs, probs_of, picked):
    half = 2 * PEER
    slots = CHUNK * PEER
    width = xs.shape[3]
    for plane in range(n):
        for pair in range(2):
            spots = pl.ds(pair * half, half)
            pick = hot(tgt_x, plane, pair)
            rows = x[plane * 2 + pair]
            got = dot(pick, rows[:, pl.ds(0, width)]).astype(BF16)
            local = rel[plane, pl.ds(pair * 2 * SRC, 2 * SRC), :].astype(F32)
            probs = rows[:, pl.ds(width, LANES)].astype(F32)
            got_g = dot(hot(tgt_g, plane, pair), g[plane * 2 + pair][...]).astype(BF16)
            for e in range(2):
                part = slice(e * half, (e + 1) * half)
                xs[e, plane, spots, :] = got[part]
                picked[e, pl.ds(plane * slots + pair * half, half), :] = got_g[part]
                for i in range(2):
                    at = e * half + i * PEER
                    gs[e, pair * 2 + i, plane] = got_g[at : at + PEER]
                mine = jnp.where(local == e, probs, 0.0).astype(BF16)
                col = jnp.sum(dot(pick[part], mine), axis=1, keepdims=True)
                probs_of[e, pl.ds(plane * slots + pair * half, half), :] = jnp.broadcast_to(col, (half, LANES))


def products(rows, picked, p, wg, wu, wd):
    h = dot(rows, wg)
    u = dot(rows, wu)
    s = 1.0 / (1.0 + jnp.exp(-h))
    hs = h * s
    a = hs * u
    wp = p * (u * s * (1.0 + h * (1.0 - s)))
    return tuple(v.astype(BF16) for v in (p * a, a, wp, p * hs, dot(picked, wd, NT)))


def stage_kernel(n, tgt_x, tgt_g, rel, *refs):
    x, g, (wg, wu, wd) = refs[: 2 * n], refs[2 * n : 4 * n], refs[4 * n : 4 * n + 3]
    xs, pa, ab, wp, hp, gs, dap, probs_of, picked = refs[-9:]
    slots = CHUNK * PEER
    width, ff = wg.shape[1], wg.shape[2]
    e = pl.program_id(0)

    @pl.when(e == 0)
    def _():
        pick_rows(n, tgt_x, tgt_g, rel, x, g, xs, gs, probs_of, picked)

    rows = xs[e].reshape(n * slots, width)
    *made, back = products(rows, picked[e], probs_of[e][:, :1], wg[0], wu[0], wd[0])
    for out, value in zip((pa, ab, wp, hp), made):
        out[0] = value.reshape(n, slots, ff)
    for plane in range(n):
        for i in range(CHUNK):
            at = plane * slots + i * PEER
            dap[0, i, plane] = back[at : at + PEER]


def fixed(shape, *at):
    return pl.BlockSpec(shape, lambda e: at, pipeline_mode=pl.Buffered(1))


def by_expert(shape, *at):
    return pl.BlockSpec((1, *shape), lambda e: (e, *at))


def stage_pass(n, at, tables, x, g, weights, prior):
    wg, wu, wd = weights
    width, ff = wg.shape[1], wg.shape[2]
    slots = CHUNK * PEER
    by_plane = [width, ff, ff, ff, ff]
    by_line = [width, ff]
    held = [] if prior is None else list(prior)
    before = 3 + len(x) + len(g) + 3
    return pl.pallas_call(
        functools.partial(stage_kernel, n),
        grid=(2,),
        in_specs=[fixed((n, CHUNK, 2 * SRC), at, 0, 0)] * 2
        + [fixed((n, CHUNK * SRC, LANES), at, 0, 0)]
        + [fixed(v.shape, 0, 0) for v in (*x, *g)]
        + [by_expert(w.shape[1:], 0, 0) for w in weights]
        + [pl.BlockSpec(memory_space=pl.ANY)] * len(held),
        out_specs=[fixed((2, n, slots, width), 0, at, 0, 0)]
        + [by_expert((n, slots, ff), at, 0, 0)] * 4
        + [fixed((2, 4, n, PEER, width), 0, 0, at, 0, 0), by_expert((4, n, PEER, ff), 0, at, 0, 0)],
        out_shape=[jax.ShapeDtypeStruct((2, 4, slots, w), BF16) for w in by_plane]
        + [jax.ShapeDtypeStruct((2, 4, 4, PEER, w), BF16) for w in by_line],
        scratch_shapes=[pltpu.VMEM((2, n * slots, LANES), F32), pltpu.VMEM((2, n * slots, width), BF16)],
        input_output_aliases={before + i: i for i in range(len(held))},
        compiler_params=pltpu.CompilerParams(vmem_limit_bytes=VMEM),
        cost_estimate=pl.CostEstimate(flops=1 << 28, bytes_accessed=1 << 19, transcendentals=0),
        name="stage",
    )(*tables, *x, *g, *weights, *held)


def turn_kernel(wg, wu, out):
    ff = wg.shape[2]
    out[0, pl.ds(0, ff), :] = wg[0].T
    out[0, pl.ds(ff, ff), :] = wu[0].T


def turn_pass(wg, wu):
    width, ff = wg.shape[1], wg.shape[2]
    return pl.pallas_call(
        turn_kernel,
        grid=(2,),
        in_specs=[by_expert((width, ff), 0, 0)] * 2,
        out_specs=by_expert((2 * ff, width), 0, 0),
        out_shape=jax.ShapeDtypeStruct((2, 2 * ff, width), BF16),
        compiler_params=pltpu.CompilerParams(vmem_limit_bytes=VMEM),
        cost_estimate=pl.CostEstimate(flops=1 << 28, bytes_accessed=1 << 19, transcendentals=0),
        name="turn",
    )(wg, wu)


def held_copies(held, kept, wt_hbm, wt, sem):
    copies = [(wt_hbm.at[e], wt.at[e]) for e in range(2)]
    for i, (src, dst) in enumerate(zip(held, kept)):
        for part in (pl.ds(0, 1), pl.ds(2, 2)):
            at = (slice(None), slice(None), part) if i == 3 else (slice(None), part)
            copies.append((src.at[at], dst.at[at]))
    return [pltpu.make_async_copy(src, dst, sem.at[i]) for i, (src, dst) in enumerate(copies)]


def tail_kernel(place, tgt_x, tgt_g, rel_x, tgt, rel, x_lo, x_hi, g_lo, g_hi, wg, wu, wd, wt_hbm, *refs):
    held = refs[3:7]
    xs, pa, gs, dhu, act, wt, ab, wp, hp, dap, probs_of, picked, dxs, qs, sem = refs[7:]
    kept = (ab, wp, hp, dap)
    half = 2 * PEER
    slots = CHUNK * PEER
    width, ff = wg.shape[1], wg.shape[2]
    step = pl.program_id(0)

    @pl.when(step == 0)
    def _():
        for copy in held_copies(held, kept, wt_hbm, wt, sem)[2:]:
            copy.start()
        pick_rows(1, tgt_x, tgt_g, rel_x, (x_lo, x_hi), (g_lo, g_hi), xs, gs, probs_of, picked)

    @pl.when(step == 1)
    def _():
        for copy in held_copies(held, kept, wt_hbm, wt, sem)[:2]:
            copy.start()

    @pl.when(step < 2)
    def _():
        made = products(xs[step, 0], picked[step], probs_of[step][:, :1], wg[0], wu[0], wd[0])
        pa[0, 0] = made[0]
        for out, value in zip((ab, wp, hp), made[1:4]):
            out[step, 1] = value
        for i in range(CHUNK):
            dap[step, i, 1] = made[4][i * PEER : (i + 1) * PEER]

    @pl.when(step == 2)
    def _():
        for copy in held_copies(held, kept, wt_hbm, wt, sem):
            copy.wait()

    @pl.when(step >= 2)
    def _():
        k = step - 2
        for e in range(2):
            back = dap[e, k].astype(F32).reshape(slots, ff)
            q = jnp.sum(ab[e, k].astype(F32) * back, axis=1, keepdims=True)
            dhu[e, :, pl.ds(0, ff)] = (back * wp[e, k].astype(F32)).astype(BF16)
            dhu[e, :, pl.ds(ff, ff)] = (back * hp[e, k].astype(F32)).astype(BF16)
            wide = jnp.broadcast_to(q, (slots, LANES)).astype(BF16)
            for pair in range(2):
                qs[pair, pl.ds(e * half, half), :] = wide[pair * half : (pair + 1) * half]
        for e in range(2):
            dx = dot(dhu[e], wt[e]).astype(BF16)
            for pair in range(2):
                dxs[pair, pl.ds(e * half, half), :] = dx[pair * half : (pair + 1) * half]
        for pair in range(2):
            pick = hot(tgt, 0, pair)
            rows = dot(pick, dxs[pair], TN).astype(BF16)
            local = rel[0, pl.ds(pair * 2 * SRC, 2 * SRC), :].astype(F32)
            ext = jnp.zeros(local.shape, F32)
            for e in range(2):
                part = slice(e * half, (e + 1) * half)
                ext = ext + jnp.where(local == e, dot(pick[part], qs[pair, pl.ds(e * half, half), :], TN), 0.0)
            ext = ext.astype(BF16)
            for i in range(2):
                part = slice(i * SRC, (i + 1) * SRC)
                y = place[4 + pair * 2 + i]
                act[0, y, :, pl.ds(0, width)] = rows[part]
                act[0, y, :, pl.ds(width, LANES)] = ext[part]


def tail_pass(place, tables, x, g, weights, wt, made):
    tgt_x, tgt_g, rel = tables
    wg, wu, wd = weights
    width, ff = wg.shape[1], wg.shape[2]
    slots = CHUNK * PEER
    xs, pa, ab, wp, hp, gs, dap = made
    once = pl.Buffered(1)
    kept = lambda shape, *at: pl.BlockSpec(shape, lambda i, p: at, pipeline_mode=once)
    plane = lambda i: jnp.maximum(i - 2, 0)
    expert = lambda i: jnp.minimum(i, 1)
    of_plane = lambda *shape: pl.BlockSpec((1, *shape), lambda i, p: (plane(i), 0, 0))
    of_expert = lambda w: pl.BlockSpec((1, *w.shape[1:]), lambda i, p: (expert(i), 0, 0))
    anywhere = pl.BlockSpec(memory_space=pl.ANY)
    return pl.pallas_call(
        tail_kernel,
        grid_spec=pltpu.PrefetchScalarGridSpec(
            num_scalar_prefetch=1,
            grid=(6,),
            in_specs=[
                kept((1, CHUNK, 2 * SRC), 1, 0, 0),
                kept((1, CHUNK, 2 * SRC), 1, 0, 0),
                kept((1, CHUNK * SRC, LANES), 1, 0, 0),
                of_plane(CHUNK, 2 * SRC),
                of_plane(CHUNK * SRC, LANES),
            ]
            + [kept(v.shape, 0, 0) for v in (*x, *g)]
            + [of_expert(w) for w in weights]
            + [anywhere] * 8,
            out_specs=[
                kept((2, 1, slots, width), 0, 1, 0, 0),
                pl.BlockSpec((1, 1, slots, ff), lambda i, p: (expert(i), 1, 0, 0)),
                kept((2, 4, 1, PEER, width), 0, 0, 1, 0, 0),
                pl.BlockSpec((2, slots, 2 * ff), lambda i, p: (0, plane(i), 0)),
                pl.BlockSpec((1, 4, SRC, width + LANES), lambda i, p: (p[plane(i)], 0, 0, 0)),
            ],
            scratch_shapes=[
                pltpu.VMEM(wt.shape, BF16),
                pltpu.VMEM(ab.shape, BF16),
                pltpu.VMEM(wp.shape, BF16),
                pltpu.VMEM(hp.shape, BF16),
                pltpu.VMEM(dap.shape, BF16),
                pltpu.VMEM((2, slots, LANES), F32),
                pltpu.VMEM((2, slots, width), BF16),
                pltpu.VMEM((2, 4 * PEER, width), BF16),
                pltpu.VMEM((2, 4 * PEER, LANES), BF16),
                pltpu.SemaphoreType.DMA((10,)),
            ],
        ),
        out_shape=[jax.ShapeDtypeStruct(v.shape, BF16) for v in (xs, pa, gs)]
        + [
            jax.ShapeDtypeStruct((2, 4 * slots, 2 * ff), BF16),
            jax.ShapeDtypeStruct((4, 4, SRC, width + LANES), BF16),
        ],
        input_output_aliases={14: 0, 15: 1, 16: 2},
        compiler_params=pltpu.CompilerParams(vmem_limit_bytes=VMEM),
        cost_estimate=pl.CostEstimate(flops=14 << 30, bytes_accessed=32 << 20, transcendentals=0),
        name="tail",
    )(place, tgt_x, tgt_g, rel, tgt_x, rel, *x, *g, wg, wu, wd, wt, xs, pa, gs, ab, wp, hp, dap)


def place_chunks(where, total, outs, step):
    my_x, my_c = where[0], where[1]
    for ahead in range(4):
        for own in range(2):
            core = my_c if own else 1 - my_c
            piece = lax.rem(my_x + ahead, 4) * 2 + core
            start = pl.multiple_of(piece * step, step)
            outs[own][ahead, 0] = total[pl.ds(start, step), :].astype(BF16)


def down_kernel(where, pa, gs, other, own, total):
    total[...] = dot(pa[0], gs[0], TN)
    place_chunks(where, total, (other, own), total.shape[0] // 8)


def up_kernel(where, xs, dhu, other, own, total):
    total[...] = dot(xs[0], dhu[0], TN)
    place_chunks(where, total, (other, own), total.shape[0] // 8)


def weight_pass(body, where, args, rows, cols, name):
    slots = args[0].shape[1]
    step = rows // 8
    out = jax.ShapeDtypeStruct((4, 2, step, cols), BF16)
    out_spec = pl.BlockSpec((4, 1, step, cols), lambda e: (0, e, 0, 0))
    return pl.pallas_call(
        body,
        grid=(2,),
        in_specs=[pl.BlockSpec(memory_space=pltpu.SMEM)]
        + [pl.BlockSpec((1, slots, a.shape[2]), lambda e: (e, 0, 0)) for a in args],
        out_specs=[out_spec, out_spec],
        out_shape=[out, out],
        scratch_shapes=[pltpu.VMEM((rows, cols), F32)],
        compiler_params=pltpu.CompilerParams(vmem_limit_bytes=VMEM),
        cost_estimate=pl.CostEstimate(flops=4 * slots * rows * cols, bytes_accessed=16 << 20, transcendentals=0),
        name=name,
    )(where, *args)


def along_x(by):
    return [(x * 2 + c, (x + by) % 4 * 2 + c) for x in range(4) for c in range(2)]


def swap_cores(other):
    return lax.ppermute(other, "dp", [(x * 2 + c, x * 2 + 1 - c) for x in range(4) for c in range(2)])


def both(own, got, *at):
    return own[at].astype(F32) + got[at].astype(F32)


def send_far(own, got):
    return (
        lax.ppermute(both(own, got, 2, 0).astype(BF16), "dp", along_x(1)),
        lax.ppermute(both(own, got, 2, 1).astype(BF16), "dp", along_x(-1)),
    )


def send_near(own, got, far):
    ahead = jnp.stack([both(own, got, 1, 0) + far[0].astype(F32), both(own, got, 1, 1)]).astype(BF16)
    back = jnp.stack([both(own, got, 3, 0), both(own, got, 3, 1) + far[1].astype(F32)]).astype(BF16)
    ahead, back = lax.ppermute(ahead, "dp", along_x(1)), lax.ppermute(back, "dp", along_x(-1))
    return both(own, got, 0) + ahead.astype(F32) + back.astype(F32)


def along_y(by):
    return [(z * 4 + y, z * 4 + (y + by) % 4) for z in range(4) for y in range(4)]


def along_z(by):
    return [(z * 4 + y, (z + by) % 4 * 4 + y) for z in range(4) for y in range(4)]


def send(value, route):
    return lax.ppermute(value, "expert", route)


def gather_line(block, ring):
    half = block.shape[0] // 2
    back, ahead = send(block, ring(1)), send(block, ring(-1))
    far = [send(back[:half], ring(1)), send(ahead[half:], ring(-1))]
    return jnp.concatenate([block, *far], axis=0), jnp.concatenate([back, ahead], axis=0)


def tables(ids, first, my_z, my_y):
    mine = first + jnp.arange(2, dtype=jnp.int32)
    ids = ids.reshape(4, 4, SRC, TOP)
    ids = jnp.roll(ids, (-my_z, -my_y), (0, 1))
    ids = jnp.stack([ids[0], ids[2], ids[3], ids[1]])
    ids = jnp.stack([ids[:, 0], ids[:, 2], ids[:, 3], ids[:, 1]], axis=1)
    hit = jnp.any(ids[None] == mine[:, None, None, None, None], axis=4)
    before = jnp.triu(jnp.ones((SRC, SRC), BF16), 1)
    rank = jnp.einsum("ezyr,rs->ezys", hit.astype(BF16), before, preferred_element_type=F32).astype(jnp.int32)
    slot = jnp.where(hit, rank, -2 * PEER)

    def by_pairs(t):
        t = t.reshape(2, 4, 2, 2, SRC) + jnp.arange(2, dtype=jnp.int32)[:, None] * PEER
        return jnp.transpose(t, (1, 0, 2, 3, 4)).reshape(4, CHUNK, 2 * SRC)

    rel = jnp.pad((ids - first).reshape(4, 4 * SRC, TOP), ((0, 0), (0, 0), (0, LANES - TOP)), constant_values=-1)
    return by_pairs(slot), by_pairs(jnp.swapaxes(slot, 1, 2)), rel.astype(BF16)


def on_device(activations, out_grad, gate_probs, expert_ids, w_gate, w_up, w_down):
    my_index = lax.axis_index("expert")
    dp_index = lax.axis_index("dp")
    width = activations.shape[1]
    ff = w_gate.shape[2]
    my_z, my_y = my_index // 4, my_index % 4
    rows = jnp.concatenate([activations, jnp.pad(gate_probs, ((0, 0), (0, LANES - TOP)))], axis=1)
    tgt_x, tgt_g, rel = tables(expert_ids, my_index * 2, my_z, my_y)
    weights = (w_gate, w_up, w_down)
    x_own, g_own = lax.optimization_barrier((gather_line(rows, along_y), gather_line(out_grad, along_z)))
    (x_lo, x_hi), (g_lo, g_hi) = x_own, g_own
    onward = (
        send(x_hi, along_z(1)),
        send(x_lo, along_z(-1)),
        send(g_hi, along_y(1)),
        send(g_lo, along_y(-1)),
    )
    turned = turn_pass(w_gate, w_up)
    made = stage_pass(1, 0, (tgt_x, tgt_g, rel), x_own, g_own, weights, None)
    x_lo, x_hi, g_lo, g_hi, onward, turned, made = lax.optimization_barrier(
        (x_lo, x_hi, g_lo, g_hi, onward, turned, made)
    )
    x_near = send(x_lo, along_z(1)), onward[0], onward[1], send(x_hi, along_z(-1))
    g_near = send(g_lo, along_y(1)), onward[2], onward[3], send(g_hi, along_y(-1))
    x_far = send(onward[1], along_z(-1)), send(onward[0], along_z(1))
    g_far = send(onward[3], along_y(-1)), send(onward[2], along_y(1))
    made = stage_pass(2, 1, (tgt_x, tgt_g, rel), x_near, g_near, weights, made)
    away = jnp.array([0, 2, 3, 1], jnp.int32)
    place = jnp.concatenate([(my_z + away) % 4, (my_y + away) % 4]).astype(jnp.int32)
    xs, pa, gs, dhu, act = tail_pass(place, (tgt_x, tgt_g, rel), x_far, g_far, weights, turned, made)
    act_sum = lax.psum_scatter(act.reshape(16 * SRC, -1), "expert", scatter_dimension=0, tiled=True)
    where = jnp.stack([dp_index // 2, dp_index % 2]).astype(jnp.int32)
    flat = lambda v: v.reshape(2, 16 * PEER, -1)
    up = weight_pass(up_kernel, where, (flat(xs), dhu), width, 2 * ff, "up_grad")
    down = weight_pass(down_kernel, where, (flat(pa), flat(gs)), ff, width, "down_grad")
    got_up, got_down = swap_cores(up[0]), swap_cores(down[0])
    far_up = send_far(up[1], got_up)
    got_down, far_up = lax.optimization_barrier((got_down, far_up))
    far_down = send_far(down[1], got_down)
    grad_both = send_near(up[1], got_up, far_up)
    grad_down = send_near(down[1], got_down, far_down)
    return (
        act_sum[:, :width],
        act_sum[:, width : width + TOP].astype(F32),
        grad_both[:, :, :ff].astype(BF16),
        grad_both[:, :, ff:].astype(BF16),
        grad_down.astype(BF16),
    )


def solution(mesh):
    placed = (
        P(("dp", "expert"), None),
        P(("dp", "expert"), None),
        P(("dp", "expert"), None),
        P("dp", None),
        P("expert", None, None),
        P("expert", None, None),
        P("expert", None, None),
    )
    return jax.shard_map(
        on_device,
        mesh=mesh,
        in_specs=placed,
        out_specs=(
            P(("dp", "expert"), None),
            P(("dp", "expert"), None),
            P("expert", "dp", None),
            P("expert", "dp", None),
            P("expert", "dp", None),
        ),
        check_vma=False,
    )
```
